32 devices in a mesh: queue: 16 (over z, y, core), space: 2 (over x).
Axes of the slice: x: 2, y: 2, z: 4, core: 2. Of those that a mesh axis runs over, the one named last changes fastest.
Arguments:
- latents: float32 [16, 96, 16], P('queue', 'space'), may hold values from -6 to 6
- fresh_noise: float32 [2, 96, 16], P(None, 'space'), may hold values from -6 to 6
- levels: int32 [16], replicated, may hold values from 1 to 1000, as said below
- modulation_weight: bfloat16 [256, 6912], P(None, 'space'), may hold values from -0.375 to 0.375
- embed_weight: bfloat16 [16, 1152], replicated, may hold values from -1.5 to 1.5
- attention_weights: bfloat16 [8, 1152, 1152], P(None, 'space')
- final_weight: bfloat16 [1152, 16], replicated, may hold values from -0.1875 to 0.1875
Outputs:
- queue_after: float32 [16, 96, 16], P('queue', 'space')
- velocity: float32 [2, 16, 96, 16], P(None, 'queue', 'space')
The draws below stay inside these ranges and needn't reach their ends.
Inputs may be any that keep to these rules, and one draw needn't show every extreme that they name: levels rise strictly along the queue, and the last one is 1000.
All inputs are finite; a program needn't handle non-finite values.
Results may differ from the reference program's by a relative error of at most 0.034.
Values may be sent and summed in bfloat16 or wider, within the bound.
No kernel may reach another device: no remote copies, remote signals or barrier semaphores. Data moves between devices by JAX's collectives and lax.ppermute only.
A program may use at most 64 MiB of HBM per device.

```python
import math
import jax
import jax.numpy as jnp
from jax import lax

D = 1152
HEAD = 72
HEADS = 16
CH = 16
FREQ = 256
STEPS = 2
REACH = 4
LEVELS = 1000
INNER = 1152
NB = 16
S_ALL = 96
HGROUPS = 2


def draw_levels(key, part):
    key = jax.random.fold_in(key, 7)
    increments = jax.random.randint(key, (NB - 1,), 1, LEVELS // NB + 1)
    rising = jnp.cumsum(increments)
    return jnp.concatenate([rising, jnp.full((1,), LEVELS, jnp.int32)]).astype(jnp.int32)


def draw_attention_weights(key, part):
    key = jax.random.fold_in(key, 11)
    base = jax.random.normal(key, (8, INNER, D), jnp.float32)
    input_scale = D ** (-0.5)
    output_scale = INNER ** (-0.5)
    matrices = [base[index] * (output_scale if index % 4 == 3 else input_scale) for index in range(8)]
    return jnp.stack(matrices, 0).astype(jnp.bfloat16)


def block_scale(own_key, shape, shards, smallest, largest):
    gain, own = 1.0, jax.random.fold_in(own_key, 6)
    for axis_at, shards_of in shards:
        heights = jnp.exp(jax.random.uniform(jax.random.fold_in(own, axis_at), (shards_of,), jnp.float32, smallest / len(shards), largest / len(shards)))
        gain = gain * jnp.repeat(heights, shape[axis_at] // shards_of).reshape([-1 if axis == axis_at else 1 for axis in range(len(shape))])
    return gain


def scatter_about(key, dims, deviation, bound, pieces=(), held_as=jnp.bfloat16):
    gain = block_scale(key, dims, pieces, -0.22, 0.18) if pieces else 1.0
    drawn = jax.random.normal(key, dims, jnp.float32) * deviation * gain
    return jnp.minimum(jnp.maximum(drawn, -bound), bound).astype(held_as)


def setup_inputs(seed: int = 0) -> dict:
    seeds = jax.random.split(jax.random.key(seed), 8)
    return {
        "latents": scatter_about(seeds[0], (NB, S_ALL, CH), 1.0, 6.0, ((0, 16), (1, 2)), jnp.float32),
        "fresh_noise": scatter_about(seeds[1], (STEPS, S_ALL, CH), 1.0, 6.0, ((1, 2),), jnp.float32),
        "levels": draw_levels(jax.random.fold_in(seeds[7], 71), 0),
        "modulation_weight": scatter_about(seeds[3], (FREQ, 6 * D), FREQ ** -0.5, 0.375, ((1, 2),)),
        "embed_weight": scatter_about(seeds[4], (CH, D), CH ** -0.5, 1.5),
        "attention_weights": draw_attention_weights(jax.random.fold_in(seeds[7], 71), 0),
        "final_weight": scatter_about(seeds[6], (D, CH), D ** -0.5, 0.1875),
    }


def layer_norm(values):
    average = lax.optimization_barrier(jnp.mean(values, -1, keepdims=True))
    centred = values - average
    variance = lax.optimization_barrier(jnp.mean(centred * centred, -1, keepdims=True))
    return centred * lax.rsqrt(variance + 1e-06)

def time_features(level_values):
    times = level_values.astype(jnp.float32) / LEVELS
    half_size = FREQ // 2
    frequency = jnp.exp(-math.log(10000.0) * jnp.arange(half_size).astype(jnp.float32) / half_size)
    angles = (times * 1000.0)[:, None] * frequency[None, :]
    return jnp.concatenate([jnp.cos(angles), jnp.sin(angles)], -1).astype(jnp.bfloat16)

def spatial_attend(query, key_rows, values):
    scores = jnp.einsum('qhd,khd->hqk', query.astype(jnp.float32), key_rows.astype(jnp.float32)) * (1.0 / math.sqrt(HEAD))
    probabilities = jax.nn.softmax(scores, axis=-1).astype(jnp.bfloat16)
    return jnp.einsum('hqk,khd->qhd', probabilities.astype(jnp.float32), values.astype(jnp.float32)).astype(jnp.bfloat16)

def temporal_attend(query, key_rows, values, usable):
    scores = jnp.einsum('shd,gshd->shg', query.astype(jnp.float32), key_rows.astype(jnp.float32)) * (1.0 / math.sqrt(HEAD))
    scores = jnp.where(usable[None, None, :], scores, -1e+30)
    probabilities = jax.nn.softmax(scores, axis=-1).astype(jnp.bfloat16)
    return jnp.einsum('shg,gshd->shd', probabilities.astype(jnp.float32), values.astype(jnp.float32)).astype(jnp.bfloat16)

def grouped_output(attended, exit_weight):
    group_width = INNER // HGROUPS
    total = jnp.zeros((attended.shape[0], exit_weight.shape[1]), jnp.float32)
    for group in range(HGROUPS):
        first = group * group_width
        product = jnp.dot(attended[:, first:first + group_width], exit_weight[first:first + group_width, :], preferred_element_type=jnp.float32)
        total = total + lax.optimization_barrier(product.astype(jnp.bfloat16)).astype(jnp.float32)
    return total

def denoise(current, conditioning, attention_weights, embed_weight, final_weight):
    block_count, token_count, channels = current.shape
    width = embed_weight.shape[1]
    conditioning = conditioning[:, None, :]

    def project(index, source):
        result = jnp.dot(source.reshape(-1, width), attention_weights[index].T, preferred_element_type=jnp.float32)
        return result.astype(jnp.bfloat16).reshape(block_count, token_count, HEADS, HEAD)
    stream_in = jnp.dot(current.astype(jnp.bfloat16).reshape(-1, channels), embed_weight, preferred_element_type=jnp.float32)
    stream_in = stream_in.reshape(block_count, token_count, width)
    normed = (layer_norm(stream_in) * (1.0 + conditioning[..., width:2 * width]) + conditioning[..., 0:width]).astype(jnp.bfloat16)
    spatial = lax.map(lambda group: spatial_attend(group[0], group[1], group[2]), (project(0, normed), project(1, normed), project(2, normed)))
    spatial_sum = grouped_output(spatial.reshape(-1, INNER), attention_weights[3]).reshape(block_count, token_count, width)
    stream_mid = stream_in + conditioning[..., 2 * width:3 * width] * spatial_sum
    normed_temporal = (layer_norm(stream_mid) * (1.0 + conditioning[..., 4 * width:5 * width]) + conditioning[..., 3 * width:4 * width]).astype(jnp.bfloat16)
    temporal_query = project(4, normed_temporal)
    key_padded = jnp.pad(project(5, normed_temporal), ((REACH, REACH), (0, 0), (0, 0), (0, 0)))
    value_padded = jnp.pad(project(6, normed_temporal), ((REACH, REACH), (0, 0), (0, 0), (0, 0)))

    def one_block(index):
        key_rows = lax.dynamic_slice_in_dim(key_padded, index, 2 * REACH + 1, 0)
        values = lax.dynamic_slice_in_dim(value_padded, index, 2 * REACH + 1, 0)
        offsets = jnp.arange(2 * REACH + 1).astype(jnp.int32) - REACH + index
        usable = (offsets >= 0) & (offsets < block_count)
        query = lax.dynamic_index_in_dim(temporal_query, index, 0, keepdims=False)
        return temporal_attend(query, key_rows, values, usable)
    temporal = lax.map(one_block, jnp.arange(block_count).astype(jnp.int32))
    temporal_sum = grouped_output(temporal.reshape(-1, INNER), attention_weights[7]).reshape(block_count, token_count, width)
    stream_out = stream_mid + conditioning[..., 5 * width:6 * width] * temporal_sum
    velocity = jnp.dot(layer_norm(stream_out).astype(jnp.bfloat16).reshape(-1, width), final_weight, preferred_element_type=jnp.float32)
    return velocity.reshape(block_count, token_count, channels)

def reference(latents, fresh_noise, levels, modulation_weight, embed_weight, attention_weights, final_weight):
    conditioning = jnp.dot(time_features(levels), modulation_weight, preferred_element_type=jnp.float32)
    lower = jnp.concatenate([jnp.zeros((1,), jnp.int32), levels[:-1].astype(jnp.int32)])
    step_size = (lower - levels.astype(jnp.int32)).astype(jnp.float32) / LEVELS
    current = latents
    velocities = []
    for iteration in range(STEPS):
        velocity = denoise(current, conditioning, attention_weights, embed_weight, final_weight)
        velocities.append(velocity)
        updated = current + step_size[:, None, None] * velocity
        current = jnp.concatenate([updated[1:], fresh_noise[iteration][None]], 0)
    return (current, jnp.stack(velocities, 0))
```

```python
import functools
import math

import jax
import jax.numpy as jnp
from jax import lax
from jax.experimental import pallas as pl
from jax.experimental.pallas import tpu as pltpu
from jax.sharding import PartitionSpec as P

HEAD = 72
FREQ = 256
STEPS = 2
REACH = 4
LEVELS = 1000
CH = 16
PIECES = 6
LANES = 128
SLOTS = 32
GROUP = 8
MIB = 1024 * 1024
F32 = jnp.float32
BF16 = jnp.bfloat16
EXACT = lax.Precision.HIGHEST


def time_features(level_values):
    times = level_values.astype(F32) / LEVELS
    half_size = FREQ // 2
    frequency = jnp.exp(-math.log(10000.0) * jnp.arange(half_size).astype(F32) / half_size)
    angles = (times * 1000.0)[:, None] * frequency[None, :]
    return jnp.concatenate([jnp.cos(angles), jnp.sin(angles)], -1).astype(BF16)


def layer_norm(values):
    average = jnp.mean(values, -1, keepdims=True)
    centred = values - average
    variance = jnp.mean(centred * centred, -1, keepdims=True)
    return centred * lax.rsqrt(variance + 1e-06)


def iota(shape, dimension):
    return lax.broadcasted_iota(jnp.int32, shape, dimension)


def ones_where(condition, dtype=BF16):
    return jnp.where(condition, 1.0, 0.0).astype(dtype)


def rows_by(left, right, precision=None):
    return lax.dot_general(
        left, right, (((1,), (1,)), ((), ())), precision=precision, preferred_element_type=F32
    )


def product(left, right, precision=None):
    return jnp.dot(left, right, precision=precision, preferred_element_type=F32)


def over(count, body):
    if count <= 16:
        for at in range(count):
            body(at)
    else:
        lax.fori_loop(0, count, lambda at, _: body(at), None)


def rows_at(at, size):
    if isinstance(at, int):
        return slice(at * size, (at + 1) * size)
    return pl.ds(pl.multiple_of(at * size, size), size)


def piece_of(mods_ref, piece, share):
    blocks = mods_ref.shape[0] // PIECES
    return jnp.concatenate([mods_ref[piece * blocks : (piece + 1) * blocks, :]] * share, 0)


def scaled(latents, cov):
    x = latents.astype(BF16).astype(F32)
    variance = jnp.sum(x * product(x, cov, EXACT), -1, keepdims=True)
    return x * lax.rsqrt(jnp.maximum(variance, 0.0) + 1e-06)


def loader_kernel(first, weights_ref, held_ref, semaphores):
    copies = [
        pltpu.make_async_copy(weights_ref.at[first + at], held_ref.at[at], semaphores.at[at])
        for at in range(held_ref.shape[0])
    ]
    for copy in copies:
        copy.start()
    for copy in copies:
        copy.wait()


def opening_kernel(
    levels_hbm, weight_hbm, latents_hbm, embed_hbm, vectors_ref, sizes_ref, packed_ref, embed_ref,
    levels_ref, weight_ref, latents_ref, semaphores,
):
    pairs = (
        (levels_hbm, levels_ref),
        (latents_hbm, latents_ref),
        (weight_hbm, weight_ref),
        (embed_hbm, embed_ref),
    )
    copies = [
        pltpu.make_async_copy(source, target, semaphores.at[at])
        for at, (source, target) in enumerate(pairs)
    ]
    for copy in copies:
        copy.start()
    copies[0].wait()
    blocks = vectors_ref.shape[0]
    shape = (blocks, FREQ // 2)
    frequency = jnp.exp(-math.log(10000.0) * iota(shape, 1).astype(F32) / (FREQ // 2))
    row = iota(shape, 0)
    level = jnp.zeros(shape, jnp.int32)
    below = jnp.zeros(shape, jnp.int32)
    for block in range(blocks):
        level = jnp.where(row == block, levels_ref[block], level)
        if block:
            below = jnp.where(row == block, levels_ref[block - 1], below)
    sizes_ref[...] = (below - level).astype(F32) / LEVELS
    angles = (level.astype(F32) / LEVELS * 1000.0) * frequency
    features = jnp.concatenate([jnp.cos(angles), jnp.sin(angles)], -1).astype(BF16)
    copies[1].wait()
    shard = latents_ref.shape[2]
    gap = jnp.zeros((CH // 2, LANES // 2 - shard), F32)
    packed = [latents_ref[0, : CH // 2], gap, latents_ref[0, CH // 2 :], gap]
    packed_ref[0] = jnp.concatenate(packed, 1)
    copies[2].wait()
    vectors_ref[...] = product(features, weight_ref[...]).astype(BF16)
    copies[3].wait()


def join_kernel(*refs):
    *parts, joined_ref = refs
    count = parts[0].shape[0]
    for at, part in enumerate(parts):
        joined_ref[at * count : (at + 1) * count] = part[...]


def basis_kernel(sources, *refs):
    vectors, refs = refs[:sources], refs[sources:]
    embed_ref, weights_ref, mods_ref, cov_ref, rows_ref, last_ref = refs
    blocks = last_ref.shape[1]
    width = weights_ref.shape[2]
    if sources == 2:
        first = lax.axis_index("space") == 0
        mine, theirs = vectors[0][...].astype(F32), vectors[1][...].astype(F32)
        lower = jnp.where(first, mine, theirs)
        upper = jnp.where(first, theirs, mine)
        for piece in range(PIECES):
            part = (lower if piece < 3 else upper)[:, piece % 3 * width : (piece % 3 + 1) * width]
            mods_ref[piece * blocks : (piece + 1) * blocks, :] = part
    else:
        mods_ref[...] = vectors[0][...]
    embed = embed_ref[...].astype(F32)
    centred = embed - jnp.mean(embed, -1, keepdims=True)
    cov_ref[...] = rows_by(centred, centred, EXACT) / width
    scale = 1.0 + mods_ref[blocks : 2 * blocks, :]
    spread = [(centred * scale[block : block + 1, :]).astype(BF16) for block in range(blocks)]
    spread = jnp.concatenate(spread + [mods_ref[0:blocks, :].astype(BF16)], 0)
    for matrix in range(3):
        through = rows_by(spread, weights_ref[matrix])
        rows_ref[matrix] = through[: blocks * CH].astype(BF16)
        last_ref[matrix] = through[blocks * CH :]


def forms_kernel(rows_ref, last_ref, scores_ref, values_ref):
    blocks = scores_ref.shape[0]
    local_width = rows_ref.shape[2]
    share = (LANES - SLOTS) // CH
    head_count = local_width // HEAD
    head_mask = iota((head_count * SLOTS, local_width), 0) // SLOTS == (
        iota((head_count * SLOTS, local_width), 1) // HEAD
    )

    def per_block(block):
        def constant(matrix, size):
            row = last_ref[matrix, pl.ds(block, 1), :]
            return jnp.where(iota((size, local_width), 0) == 0, row, 0.0).astype(BF16)

        def tiled(matrix):
            rows = rows_ref[matrix, rows_at(block, CH), :]
            return jnp.concatenate([rows] * share + [constant(matrix, SLOTS)], 0)

        query = jnp.concatenate([rows_ref[0, rows_at(block, CH), :], constant(0, SLOTS - CH)], 0)
        query = jnp.where(head_mask, jnp.concatenate([query] * head_count, 0), 0.0).astype(BF16)
        scores_ref[block] = rows_by(query, tiled(1)).astype(BF16)
        values_ref[block] = tiled(2)

    over(blocks, per_block)


def spatial_kernel(first, turned, share, *refs):
    if first:
        gathered_ref, cov_ref, scores_ref, values_ref, weights_ref, *refs = refs
    else:
        gathered_ref, own_ref, cov_ref, scores_ref, values_ref, weights_ref, *refs = refs
    if first:
        term_ref, own_ref, attended_ref, asked_ref, keys_ref, natural_ref = refs
    else:
        term_ref, attended_ref, asked_ref, keys_ref = refs
    blocks = scores_ref.shape[0]
    local_width = values_ref.shape[2]
    head_count = local_width // HEAD
    devices = lax.axis_size("queue")
    tokens = share * devices
    here = lax.axis_index("queue")
    cov = cov_ref[...]

    if first:
        parts = gathered_ref.shape[0] // blocks
        shard = tokens // parts
        base = here * parts + lax.axis_index("space") if turned else 0
        filling = jnp.zeros((share * CH - CH, tokens), BF16)
        constant = ones_where(iota((SLOTS, tokens), 0) == 0)

        def keys_of(block):
            pieces = [
                gathered_ref[jnp.bitwise_xor(base, block * parts + part)] for part in range(parts)
            ]
            top = jnp.concatenate([piece[:, :shard] for piece in pieces], 1)
            low = jnp.concatenate(
                [piece[:, LANES // 2 : LANES // 2 + shard] for piece in pieces], 1
            )
            raw = jnp.concatenate([top, low], 0)
            natural_ref[block] = raw.T
            x = raw.astype(BF16).astype(F32)
            variance = jnp.sum(x * product(cov, x, EXACT), 0, keepdims=True)
            hat = x * lax.rsqrt(jnp.maximum(variance, 0.0) + 1e-06)
            keys_ref[block] = jnp.concatenate([hat.astype(BF16), filling, constant], 0)

        over(blocks, keys_of)

        def own_of(block):
            for position in range(share):
                own_ref[pl.ds(position * blocks + block, 1), :] = natural_ref[
                    block, pl.ds(position * devices + here, 1), :
                ]

        over(blocks, own_of)
    else:
        lane = iota((devices, LANES), 1) // CH
        held = gathered_ref[...].reshape(devices * blocks, LANES)
        if turned:
            row, column = iota((devices * blocks,) * 2, 0), iota((devices * blocks,) * 2, 1)
            moved = ones_where(column == row % devices * blocks + row // devices)
            held = product(moved, held).astype(BF16)
        natural = held.reshape(blocks, devices, LANES)
        for block in range(blocks):
            keys_ref[block] = jnp.concatenate(
                [
                    jnp.where((lane == position) | (lane == share), natural[block], 0.0).astype(BF16)
                    for position in range(share)
                ],
                0,
            )

    rows = share * blocks
    hat = scaled(own_ref[...], cov).astype(BF16)
    lanes = head_count * SLOTS
    wide = product(hat, ones_where(iota((CH, lanes), 1) % SLOTS == iota((CH, lanes), 0)))
    wide = jnp.where(iota((rows, lanes), 1) % SLOTS == CH, 1.0, wide).astype(BF16)
    row, column = iota((blocks * 8, rows), 0), iota((blocks * 8, rows), 1)
    moved = ones_where((row % 8 == column // blocks) & (row // 8 == column % blocks))
    asked_ref[...] = product(moved, wide)
    asked_mask = iota((head_count * 8, lanes), 0) // 8 == iota((head_count * 8, lanes), 1) // SLOTS
    head_of = iota((8, local_width), 1) // HEAD

    def asked_of(block):
        asked = jnp.concatenate([asked_ref[rows_at(block, 8), :]] * head_count, 0)
        return jnp.where(asked_mask, asked, 0.0).astype(BF16)

    def softmax(scores):
        scores = scores * (1.0 / math.sqrt(HEAD))
        raised = jnp.exp(scores - jnp.max(scores, -1, keepdims=True))
        return (raised / jnp.sum(raised, -1, keepdims=True)).astype(BF16)

    def attend(group):
        members = [group * GROUP + at for at in range(GROUP)]
        queries = [product(asked_of(block), scores_ref[block]).astype(BF16) for block in members]
        meet = product if first else rows_by
        scores = [meet(query, keys_ref[block]) for query, block in zip(queries, members)]
        shares = [softmax(score) for score in scores]
        mix = rows_by if first else product
        mixed = [mix(part, keys_ref[block]).astype(BF16) for part, block in zip(shares, members)]
        mixed = [product(part, values_ref[block]) for part, block in zip(mixed, members)]
        for part, block in zip(mixed, members):
            total = part[0:8]
            for head in range(1, head_count):
                total = jnp.where(head_of == head, part[head * 8 : (head + 1) * 8], total)
            attended_ref[rows_at(block, 8), :] = total

    over(blocks // GROUP, attend)
    row, column = iota((rows, blocks * 8), 0), iota((rows, blocks * 8), 1)
    moved = ones_where((row // blocks == column % 8) & (row % blocks == column // 8))
    attended = product(moved, attended_ref[...].astype(BF16)).astype(BF16)
    term_ref[...] = product(attended, weights_ref[3]).astype(BF16)


def summed(terms):
    total = terms[0][...].astype(F32)
    for term in terms[1:]:
        total = total + term[...].astype(F32)
    return total


def own_half(rows):
    count = rows.shape[0] // 2
    return jnp.where(lax.axis_index("space") == 0, rows[:count], rows[count:])


def attend(half, blocks, query_ref, keys_ref, values_ref, weights_ref):
    rows = query_ref.shape[0]
    local_width = query_ref.shape[1]
    head_count = local_width // HEAD
    kept = slice(0, rows)
    if half is not None:
        rows = rows // 2
        kept = pl.ds(pl.multiple_of(half * rows, rows), rows)
    query = query_ref[kept, :]
    head_of = iota((rows, local_width), 1) // HEAD
    asked = [jnp.where(head_of == head, query, 0.0).astype(BF16) for head in range(head_count)]
    scores = rows_by(jnp.concatenate(asked, 0), keys_ref[kept, :]) * (1.0 / math.sqrt(HEAD))
    row, column = iota(scores.shape, 0) % rows, iota(scores.shape, 1)
    near = (row // blocks == column // blocks) & (jnp.abs(row - column) <= REACH)
    scores = jnp.where(near, scores, -1e30)
    raised = jnp.exp(scores - jnp.max(scores, -1, keepdims=True))
    shares = (raised / jnp.sum(raised, -1, keepdims=True)).astype(BF16)
    mixed = product(shares, values_ref[kept, :])
    total = mixed[0:rows]
    for head in range(1, head_count):
        total = jnp.where(head_of == head, mixed[head * rows : (head + 1) * rows], total)
    return product(total.astype(BF16), weights_ref[3]).astype(BF16)


def temporal_kernel(share, halved, term_count, own_ref, mods_ref, embed_ref, weights_ref, *refs):
    terms, (stream_ref, term_ref, query_ref, keys_ref, values_ref) = (
        refs[:term_count],
        refs[term_count:],
    )
    blocks = mods_ref.shape[0] // PIECES
    stream = product(own_ref[...].astype(BF16), embed_ref[...])
    stream = stream + piece_of(mods_ref, 2, share) * summed(terms)
    stream_ref[...] = own_half(stream) if halved else stream
    normed = layer_norm(stream) * (1.0 + piece_of(mods_ref, 4, share)) + piece_of(mods_ref, 3, share)
    normed = normed.astype(BF16)
    query_ref[...] = rows_by(normed, weights_ref[0]).astype(BF16)
    keys_ref[...] = rows_by(normed, weights_ref[1]).astype(BF16)
    values_ref[...] = rows_by(normed, weights_ref[2]).astype(BF16)
    half = 1 - lax.axis_index("space") if halved else None
    term_ref[...] = attend(half, blocks, query_ref, keys_ref, values_ref, weights_ref)


def kept_kernel(blocks, query_ref, keys_ref, values_ref, weights_ref, term_ref):
    half = lax.axis_index("space")
    term_ref[...] = attend(half, blocks, query_ref, keys_ref, values_ref, weights_ref)


def side_by_side(rows, blocks, share):
    parts = [rows[position * blocks : (position + 1) * blocks] for position in range(share)]
    return jnp.concatenate(parts + [jnp.zeros((blocks, LANES - share * CH), rows.dtype)], 1)


def final_kernel(share, halved, term_count, own_ref, stream_ref, mods_ref, final_ref, sizes_ref, *refs):
    terms, refs = refs[:term_count], refs[term_count:]
    blocks = mods_ref.shape[0] // PIECES
    rows = share * blocks
    own = own_half(own_ref[...]) if halved else own_ref[...]
    stream = stream_ref[...] + piece_of(mods_ref, 5, share) * summed(terms)
    velocity = rows_by(layer_norm(stream).astype(BF16), final_ref[...])
    sizes = jnp.concatenate([sizes_ref[:, :CH]] * share, 0)
    updated = own + sizes * velocity
    moved = jnp.concatenate([updated[1:], updated[:1]], 0)
    return blocks, rows, velocity, moved, refs


def between_kernel(share, term_count, iteration, noise_count, *refs):
    blocks, rows, velocity, moved, refs = final_kernel(share, False, term_count, *refs)
    noises, (cov_ref, velocity_ref, next_ref, sent_ref, noise_ref) = (
        refs[:noise_count],
        refs[noise_count:],
    )
    velocity_ref[...] = velocity
    devices = lax.axis_size("queue")
    here = lax.axis_index("queue")
    if noise_count == 2:
        mine, theirs = noises[0][iteration], noises[1][iteration]
        first = lax.axis_index("space") == 0
        noise = jnp.concatenate(
            [jnp.where(first, mine, theirs), jnp.where(first, theirs, mine)], 1
        )
    else:
        noise = noises[0][iteration]
    noise_ref[...] = noise.T
    next_ref[...] = moved
    for position in range(share):
        next_ref[(position + 1) * blocks - 1 : (position + 1) * blocks, :] = noise_ref[
            pl.ds(position * devices + here, 1), :
        ]
    hat = side_by_side(scaled(next_ref[...], cov_ref[...]), blocks, share)
    hat = jnp.where(iota((blocks, LANES), 1) == share * CH, 1.0, hat)
    sent_ref[...] = jnp.broadcast_to(hat.astype(BF16), sent_ref.shape)


def ending_kernel(share, halved, term_count, *refs):
    blocks, rows, velocity, moved, refs = final_kernel(share, halved, term_count, *refs)
    *earlier, sent_ref = refs
    pick = own_half if halved else lambda rows: rows
    sent_ref[...] = jnp.zeros_like(sent_ref)
    for at, values in enumerate([pick(ref[...]) for ref in earlier] + [velocity, moved]):
        wide = side_by_side(values, blocks, share)
        sent_ref[:, at : at + 1, :] = wide.reshape(blocks, 1, LANES)


def finish_kernel(share, arrived_ref, noise_ref, queue_ref, velocities_ref):
    devices = arrived_ref.shape[0]
    outs = []
    for at in range(STEPS + 1):
        turned = arrived_ref[:, at : at + 1, :].reshape(devices, LANES).T
        parts = [turned[position * CH : (position + 1) * CH] for position in range(share)]
        outs.append(jnp.concatenate(parts, 1))
    for step in range(STEPS):
        velocities_ref[step, 0] = outs[step]
    last = lax.axis_index("queue") == devices - 1
    queue_ref[0] = jnp.where(last, noise_ref[STEPS - 1], outs[STEPS])


def small(limit):
    return pltpu.CompilerParams(vmem_limit_bytes=limit * MIB)


def in_hbm(operands):
    return [pltpu.with_memory_space_constraint(operand, pltpu.HBM) for operand in operands]


def load(weights, first, count):
    shape = (count,) + weights.shape[1:]
    return pl.pallas_call(
        functools.partial(loader_kernel, first),
        out_shape=pltpu.VMEM(shape, weights.dtype),
        in_specs=[pl.BlockSpec(memory_space=pltpu.HBM)],
        out_specs=pl.BlockSpec(memory_space=pltpu.VMEM),
        scratch_shapes=[pltpu.SemaphoreType.DMA((count,))],
        compiler_params=small(1),
        cost_estimate=pl.CostEstimate(
            flops=0, bytes_accessed=2 * math.prod(shape), transcendentals=0
        ),
    )(*in_hbm([weights]))


def call(kernel, outs, operands, scratch=(), limit=8, held=True, from_hbm=()):
    specs = [pl.BlockSpec(memory_space=pltpu.VMEM)] * len(operands)
    specs += [pl.BlockSpec(memory_space=pltpu.HBM)] * len(from_hbm)
    if held:
        operands = [pltpu.with_memory_space_constraint(operand, pltpu.VMEM) for operand in operands]
    place = pltpu.VMEM if held else jax.ShapeDtypeStruct
    return pl.pallas_call(
        kernel,
        out_shape=[place(shape, dtype) for shape, dtype in outs],
        in_specs=specs,
        out_specs=[pl.BlockSpec(memory_space=pltpu.VMEM)] * len(outs),
        scratch_shapes=list(scratch),
        compiler_params=small(limit),
    )(*operands, *in_hbm(from_hbm))


def local(
    latents, fresh_noise, levels, modulation_weight, embed_weight, attention_weights, final_weight
):
    devices = lax.axis_size("queue")
    space_count = lax.axis_size("space")
    blocks = devices
    width = embed_weight.shape[1]
    local_width = attention_weights.shape[1]
    head_count = local_width // HEAD
    shard = latents.shape[1]
    tokens = shard * space_count
    share = tokens // devices
    rows = share * blocks
    wide_rows = share * CH + SLOTS
    run = functools.partial(call, limit=12 if rows <= 128 else 40)
    final_rows = final_weight.T
    latents = jnp.swapaxes(latents, 1, 2)
    fresh_noise = jnp.swapaxes(fresh_noise, 1, 2)

    def over_space(x):
        if space_count == 2:
            return [x, lax.ppermute(x, "space", [(0, 1), (1, 0)])]
        gathered = lax.all_gather(x, "space", axis=0, tiled=False)
        return [jnp.sum(gathered.astype(F32), 0)]

    def apart(x, mask):
        count = devices * space_count
        return lax.ppermute(x, ("queue", "space"), [(i, i ^ mask) for i in range(count)])

    def joined(*parts):
        shape = (len(parts) * parts[0].shape[0],) + parts[0].shape[1:]
        return run(join_kernel, [(shape, parts[0].dtype)], list(parts))[0]

    def after(x, *others):
        return lax.optimization_barrier((x, *others))[0]

    def basis(vectors, held):
        return run(
            functools.partial(basis_kernel, len(vectors)),
            [
                ((PIECES * blocks, width), F32),
                ((CH, CH), F32),
                ((3, blocks * CH, local_width), BF16),
                ((3, blocks, local_width), F32),
            ],
            [*vectors, embed_weight, held],
        )

    def forms(seen):
        return run(
            forms_kernel,
            [
                ((blocks, head_count * SLOTS, wide_rows), BF16),
                ((blocks, wide_rows, local_width), BF16),
            ],
            list(seen),
        )

    paired = space_count == 2 and devices == 16
    if paired:
        operands = (levels, modulation_weight, latents, embed_weight)
        vectors, sizes, packed, embed_weight = run(
            opening_kernel,
            [
                ((blocks, modulation_weight.shape[1]), BF16),
                ((blocks, LANES), F32),
                ((1, CH // 2, LANES), F32),
                (embed_weight.shape, BF16),
            ],
            [],
            [
                pltpu.SMEM(levels.shape, levels.dtype),
                pltpu.VMEM(modulation_weight.shape, modulation_weight.dtype),
                pltpu.VMEM(latents.shape, latents.dtype),
                pltpu.SemaphoreType.DMA((len(operands),)),
            ],
            from_hbm=operands,
        )
        vectors = over_space(vectors)
        spatial_weights = load(after(attention_weights, packed), 0, 4)
        gathered = joined(packed, after(apart(packed, 1), spatial_weights))
        arrivals = [apart(gathered, mask) for mask in (2, 4, 6)]
        mods, cov, *seen = basis(vectors, spatial_weights)
        arrivals[-1] = after(arrivals[-1], *seen)
        gathered = joined(gathered, *arrivals)
        arrivals = [apart(gathered, mask) for mask in (8, 16, 24)]
        scores, values = forms(seen)
        arrivals[-1] = after(arrivals[-1], scores)
        gathered = [joined(gathered, *arrivals)]
    else:
        below = jnp.concatenate([jnp.zeros((1,), levels.dtype), levels[:-1]])
        sizes = jnp.broadcast_to(((below - levels).astype(F32) / LEVELS)[:, None], (blocks, LANES))
        part = product(time_features(levels), modulation_weight)
        part = lax.all_gather(part, "space", axis=1, tiled=True).reshape(blocks, PIECES, width)
        vectors = [jnp.swapaxes(part, 0, 1).reshape(PIECES * blocks, width)]
        gap = jnp.zeros((CH // 2, LANES // 2 - shard), F32)
        packed = jnp.concatenate([latents[0, : CH // 2], gap, latents[0, CH // 2 :], gap], 1)
        noises = [lax.all_gather(fresh_noise, "space", axis=2, tiled=True)]
        gathered = lax.all_gather(packed, ("queue", "space"), axis=0, tiled=False)
        gathered = [gathered.reshape(devices * space_count, CH // 2, LANES)]
        spatial_weights = load(attention_weights, 0, 4)
        mods, cov, *seen = basis(vectors, spatial_weights)
        scores, values = forms(seen)
    temporal_weights = None
    own = None
    velocities = []
    for iteration in range(STEPS):
        first = iteration == 0
        outs = [((rows, width), BF16)]
        scratch = [
            pltpu.VMEM((blocks * 8, local_width), F32),
            pltpu.VMEM((blocks * 8, head_count * SLOTS), F32),
            pltpu.VMEM((blocks, wide_rows, tokens) if first else (blocks, tokens, LANES), BF16),
        ]
        if first:
            outs.append(((rows, CH), F32))
            scratch.append(pltpu.VMEM((blocks, tokens, CH), F32))
        spatial_term, *new = run(
            functools.partial(spatial_kernel, first, paired, share),
            outs,
            [*gathered, *([] if first else [own]), cov, scores, values, spatial_weights],
            scratch,
        )
        if first:
            (own,) = new
            held, noise, spatial_term = lax.optimization_barrier(
                (attention_weights, fresh_noise, spatial_term)
            )
            temporal_weights = load(held, 4, 4)
            if paired:
                noises = over_space(noise)
        spatial_terms = over_space(spatial_term)
        if first and paired:
            spatial_terms[-1] = after(spatial_terms[-1], noises[-1])
        last = iteration == STEPS - 1
        halved = last and paired
        held_rows = rows // 2 if halved else rows
        asked = [((rows, local_width), BF16)] * 3
        stream, temporal_term, *asked = run(
            functools.partial(temporal_kernel, share, halved, len(spatial_terms)),
            [((held_rows, width), F32), ((held_rows, width), BF16)] + (asked if halved else []),
            [own, mods, embed_weight, temporal_weights, *spatial_terms],
            [] if halved else [pltpu.VMEM(shape, dtype) for shape, dtype in asked],
        )
        temporal_terms = over_space(temporal_term)
        if halved:
            temporal_terms[:1] = run(
                functools.partial(kept_kernel, blocks),
                [((held_rows, width), BF16)],
                [*asked, temporal_weights],
            )
        operands = [own, stream, mods, final_rows, sizes, *temporal_terms]
        if not last:
            velocity, own, sent = run(
                functools.partial(
                    between_kernel, share, len(temporal_terms), iteration, len(noises)
                ),
                [
                    ((rows, CH), F32),
                    ((rows, CH), F32),
                    ((devices if paired else 1, blocks, LANES), BF16),
                ],
                operands + [*noises, cov],
                [pltpu.VMEM((tokens, CH), F32)],
            )
            velocities.append(velocity)
            if paired:
                gathered = [lax.all_to_all(sent, "queue", 0, 0, tiled=True)]
            else:
                gathered = lax.all_gather(sent[0], "queue", axis=0, tiled=False)
                gathered = [jnp.swapaxes(gathered, 0, 1).reshape(devices * blocks, LANES)]
        else:
            (sent,) = run(
                functools.partial(
                    ending_kernel, share // 2 if halved else share, halved, len(temporal_terms)
                ),
                [((blocks, 8, LANES), F32)],
                operands + velocities,
            )
    arrived = lax.all_to_all(sent, "queue", 0, 0, tiled=True)
    if paired:
        queue_out, velocity_out = run(
            functools.partial(finish_kernel, share // 2),
            [((1, CH, shard), F32), ((STEPS, 1, CH, shard), F32)],
            [arrived, fresh_noise],
            held=False,
        )
    else:
        arrived = arrived[:, : STEPS + 1, : share * CH].reshape(devices, STEPS + 1, share, CH)
        arrived = arrived.transpose(1, 3, 2, 0).reshape(STEPS + 1, CH, tokens)
        arrived = lax.dynamic_slice_in_dim(arrived, lax.axis_index("space") * shard, shard, 2)
        velocity_out = arrived[:STEPS, None]
        last = lax.axis_index("queue") == devices - 1
        queue_out = jnp.where(last, fresh_noise[STEPS - 1], arrived[STEPS])[None]
    return jnp.swapaxes(queue_out, 1, 2), jnp.swapaxes(velocity_out, 2, 3)


def solution(mesh):
    in_specs = (
        P("queue", "space", None),
        P(None, "space", None),
        P(),
        P(None, "space"),
        P(),
        P(None, "space", None),
        P(),
    )
    out_specs = (P("queue", "space", None), P(None, "queue", "space", None))
    return jax.shard_map(local, mesh=mesh, in_specs=in_specs, out_specs=out_specs, check_vma=False)
```

```python
import functools
import math

import jax
import jax.numpy as jnp
from jax import lax
from jax.experimental import pallas as pl
from jax.experimental.pallas import tpu as pltpu
from jax.sharding import PartitionSpec as P

HEAD = 72
FREQ = 256
STEPS = 2
REACH = 4
LEVELS = 1000
CH = 16
PIECES = 6
LANES = 128
SLOTS = 32
GROUP = 16
MIB = 1024 * 1024
F32 = jnp.float32
BF16 = jnp.bfloat16
EXACT = lax.Precision.HIGHEST


def time_features(level_values):
    times = level_values.astype(F32) / LEVELS
    half_size = FREQ // 2
    frequency = jnp.exp(-math.log(10000.0) * jnp.arange(half_size).astype(F32) / half_size)
    angles = (times * 1000.0)[:, None] * frequency[None, :]
    return jnp.concatenate([jnp.cos(angles), jnp.sin(angles)], -1).astype(BF16)


def layer_norm(values):
    average = jnp.mean(values, -1, keepdims=True)
    centred = values - average
    variance = jnp.mean(centred * centred, -1, keepdims=True)
    return centred * lax.rsqrt(variance + 1e-06)


def iota(shape, dimension):
    return lax.broadcasted_iota(jnp.int32, shape, dimension)


def ones_where(condition, dtype=BF16):
    return jnp.where(condition, 1.0, 0.0).astype(dtype)


def rows_by(left, right, precision=None):
    return lax.dot_general(
        left, right, (((1,), (1,)), ((), ())), precision=precision, preferred_element_type=F32
    )


def product(left, right, precision=None):
    return jnp.dot(left, right, precision=precision, preferred_element_type=F32)


def projected(rows, weights_ref):
    local_width, width = weights_ref.shape[1:]
    through = rows_by(rows, weights_ref[0:3].reshape(3 * local_width, width))
    return [through[:, at * local_width : (at + 1) * local_width] for at in range(3)]


def over(count, body):
    if count <= 16:
        for at in range(count):
            body(at)
    else:
        lax.fori_loop(0, count, lambda at, _: body(at), None)


def rows_at(at, size):
    if isinstance(at, int):
        return slice(at * size, (at + 1) * size)
    return pl.ds(pl.multiple_of(at * size, size), size)


def piece_of(mods_ref, piece, share):
    blocks = mods_ref.shape[0] // PIECES
    return jnp.concatenate([mods_ref[piece * blocks : (piece + 1) * blocks, :]] * share, 0)


def scaled(latents, cov):
    x = latents.astype(BF16).astype(F32)
    variance = jnp.sum(x * product(x, cov, EXACT), -1, keepdims=True)
    return x * lax.rsqrt(jnp.maximum(variance, 0.0) + 1e-06)


def loader_kernel(first, weights_ref, held_ref, semaphores):
    copies = [
        pltpu.make_async_copy(weights_ref.at[first + at], held_ref.at[at], semaphores.at[at])
        for at in range(held_ref.shape[0])
    ]
    for copy in copies:
        copy.start()
    for copy in copies:
        copy.wait()


def opening_kernel(
    levels_hbm, weight_hbm, latents_hbm, embed_hbm, vectors_ref, sizes_ref, packed_ref, embed_ref,
    levels_ref, weight_ref, latents_ref, semaphores,
):
    pairs = (
        (levels_hbm, levels_ref),
        (latents_hbm, latents_ref),
        (weight_hbm, weight_ref),
        (embed_hbm, embed_ref),
    )
    copies = [
        pltpu.make_async_copy(source, target, semaphores.at[at])
        for at, (source, target) in enumerate(pairs)
    ]
    for copy in copies:
        copy.start()
    copies[0].wait()
    blocks = vectors_ref.shape[0]
    shape = (blocks, FREQ // 2)
    frequency = jnp.exp(-math.log(10000.0) * iota(shape, 1).astype(F32) / (FREQ // 2))
    row = iota(shape, 0)
    level = jnp.zeros(shape, jnp.int32)
    below = jnp.zeros(shape, jnp.int32)
    for block in range(blocks):
        level = jnp.where(row == block, levels_ref[block], level)
        if block:
            below = jnp.where(row == block, levels_ref[block - 1], below)
    sizes_ref[...] = (below - level).astype(F32) / LEVELS
    angles = (level.astype(F32) / LEVELS * 1000.0) * frequency
    features = jnp.concatenate([jnp.cos(angles), jnp.sin(angles)], -1).astype(BF16)
    copies[1].wait()
    shard = latents_ref.shape[2]
    gap = jnp.zeros((CH // 2, LANES // 2 - shard), F32)
    packed = [latents_ref[0, : CH // 2], gap, latents_ref[0, CH // 2 :], gap]
    packed_ref[0] = jnp.concatenate(packed, 1)
    copies[2].wait()
    vectors_ref[...] = product(features, weight_ref[...]).astype(BF16)
    copies[3].wait()


def join_kernel(*refs):
    *parts, joined_ref = refs
    count = parts[0].shape[0]
    for at, part in enumerate(parts):
        joined_ref[at * count : (at + 1) * count] = part[...]


def basis_kernel(sources, *refs):
    vectors, refs = refs[:sources], refs[sources:]
    embed_ref, weights_ref, mods_ref, cov_ref, rows_ref, last_ref = refs
    blocks = last_ref.shape[1]
    width = weights_ref.shape[2]
    if sources == 2:
        first = lax.axis_index("space") == 0
        mine, theirs = vectors[0][...].astype(F32), vectors[1][...].astype(F32)
        lower = jnp.where(first, mine, theirs)
        upper = jnp.where(first, theirs, mine)
        for piece in range(PIECES):
            part = (lower if piece < 3 else upper)[:, piece % 3 * width : (piece % 3 + 1) * width]
            mods_ref[piece * blocks : (piece + 1) * blocks, :] = part
    else:
        mods_ref[...] = vectors[0][...]
    embed = embed_ref[...].astype(F32)
    centred = embed - jnp.mean(embed, -1, keepdims=True)
    cov_ref[...] = rows_by(centred, centred, EXACT) / width
    scale = 1.0 + mods_ref[blocks : 2 * blocks, :]
    spread = [(centred * scale[block : block + 1, :]).astype(BF16) for block in range(blocks)]
    spread = jnp.concatenate(spread + [mods_ref[0:blocks, :].astype(BF16)], 0)
    for matrix, through in enumerate(projected(spread, weights_ref)):
        rows_ref[matrix] = through[: blocks * CH].astype(BF16)
        last_ref[matrix] = through[blocks * CH :]


def forms_kernel(rows_ref, last_ref, scores_ref, values_ref):
    blocks = scores_ref.shape[0]
    local_width = rows_ref.shape[2]
    share = (LANES - SLOTS) // CH
    head_count = local_width // HEAD
    head_mask = iota((head_count * SLOTS, local_width), 0) // SLOTS == (
        iota((head_count * SLOTS, local_width), 1) // HEAD
    )

    def per_block(block):
        def constant(matrix, size):
            row = last_ref[matrix, pl.ds(block, 1), :]
            return jnp.where(iota((size, local_width), 0) == 0, row, 0.0).astype(BF16)

        def tiled(matrix):
            rows = rows_ref[matrix, rows_at(block, CH), :]
            return jnp.concatenate([rows] * share + [constant(matrix, SLOTS)], 0)

        query = jnp.concatenate([rows_ref[0, rows_at(block, CH), :], constant(0, SLOTS - CH)], 0)
        query = jnp.where(head_mask, jnp.concatenate([query] * head_count, 0), 0.0).astype(BF16)
        scores_ref[block] = rows_by(query, tiled(1)).astype(BF16)
        values_ref[block] = tiled(2)

    over(blocks, per_block)


def spatial_kernel(first, turned, share, *refs):
    if first:
        gathered_ref, cov_ref, scores_ref, values_ref, weights_ref, *refs = refs
    else:
        gathered_ref, own_ref, cov_ref, scores_ref, values_ref, weights_ref, *refs = refs
    if first:
        term_ref, own_ref, attended_ref, asked_ref, keys_ref, natural_ref = refs
    else:
        term_ref, attended_ref, asked_ref, keys_ref = refs
    blocks = scores_ref.shape[0]
    local_width = values_ref.shape[2]
    head_count = local_width // HEAD
    devices = lax.axis_size("queue")
    tokens = share * devices
    here = lax.axis_index("queue")
    cov = cov_ref[...]

    if first:
        parts = gathered_ref.shape[0] // blocks
        shard = tokens // parts
        base = here * parts + lax.axis_index("space") if turned else 0
        filling = jnp.zeros((share * CH - CH, tokens), BF16)
        constant = ones_where(iota((SLOTS, tokens), 0) == 0)

        def keys_of(block):
            pieces = [
                gathered_ref[jnp.bitwise_xor(base, block * parts + part)] for part in range(parts)
            ]
            top = jnp.concatenate([piece[:, :shard] for piece in pieces], 1)
            low = jnp.concatenate(
                [piece[:, LANES // 2 : LANES // 2 + shard] for piece in pieces], 1
            )
            raw = jnp.concatenate([top, low], 0)
            natural_ref[block] = raw.T
            x = raw.astype(BF16).astype(F32)
            variance = jnp.sum(x * product(cov, x, EXACT), 0, keepdims=True)
            hat = x * lax.rsqrt(jnp.maximum(variance, 0.0) + 1e-06)
            keys_ref[block] = jnp.concatenate([hat.astype(BF16), filling, constant], 0)

        over(blocks, keys_of)

        def own_of(block):
            for position in range(share):
                own_ref[pl.ds(position * blocks + block, 1), :] = natural_ref[
                    block, pl.ds(position * devices + here, 1), :
                ]

        over(blocks, own_of)
    else:
        lane = iota((devices, LANES), 1) // CH
        held = gathered_ref[...].reshape(devices * blocks, LANES)
        if turned:
            row, column = iota((devices * blocks,) * 2, 0), iota((devices * blocks,) * 2, 1)
            moved = ones_where(column == row % devices * blocks + row // devices)
            held = product(moved, held).astype(BF16)
        natural = held.reshape(blocks, devices, LANES)
        for block in range(blocks):
            keys_ref[block] = jnp.concatenate(
                [
                    jnp.where((lane == position) | (lane == share), natural[block], 0.0).astype(BF16)
                    for position in range(share)
                ],
                0,
            )

    rows = share * blocks
    hat = scaled(own_ref[...], cov).astype(BF16)
    lanes = head_count * SLOTS
    wide = product(hat, ones_where(iota((CH, lanes), 1) % SLOTS == iota((CH, lanes), 0)))
    wide = jnp.where(iota((rows, lanes), 1) % SLOTS == CH, 1.0, wide).astype(BF16)
    row, column = iota((blocks * 8, rows), 0), iota((blocks * 8, rows), 1)
    moved = ones_where((row % 8 == column // blocks) & (row // 8 == column % blocks))
    asked_ref[...] = product(moved, wide)
    asked_mask = iota((head_count * 8, lanes), 0) // 8 == iota((head_count * 8, lanes), 1) // SLOTS
    head_of = iota((8, local_width), 1) // HEAD

    def asked_of(block):
        asked = jnp.concatenate([asked_ref[rows_at(block, 8), :]] * head_count, 0)
        return jnp.where(asked_mask, asked, 0.0).astype(BF16)

    def softmax(scores):
        scores = scores * (1.0 / math.sqrt(HEAD))
        raised = jnp.exp(scores - jnp.max(scores, -1, keepdims=True))
        return (raised / jnp.sum(raised, -1, keepdims=True)).astype(BF16)

    def attend(group):
        members = [group * GROUP + at for at in range(GROUP)]
        queries = [product(asked_of(block), scores_ref[block]).astype(BF16) for block in members]
        meet = product if first else rows_by
        scores = [meet(query, keys_ref[block]) for query, block in zip(queries, members)]
        shares = [softmax(score) for score in scores]
        mix = rows_by if first else product
        mixed = [mix(part, keys_ref[block]).astype(BF16) for part, block in zip(shares, members)]
        mixed = [product(part, values_ref[block]) for part, block in zip(mixed, members)]
        for part, block in zip(mixed, members):
            total = part[0:8]
            for head in range(1, head_count):
                total = jnp.where(head_of == head, part[head * 8 : (head + 1) * 8], total)
            attended_ref[rows_at(block, 8), :] = total

    over(blocks // GROUP, attend)
    row, column = iota((rows, blocks * 8), 0), iota((rows, blocks * 8), 1)
    moved = ones_where((row // blocks == column % 8) & (row % blocks == column // 8))
    attended = product(moved, attended_ref[...].astype(BF16)).astype(BF16)
    term_ref[...] = product(attended, weights_ref[3]).astype(BF16)


def summed(terms):
    total = terms[0][...].astype(F32)
    for term in terms[1:]:
        total = total + term[...].astype(F32)
    return total


def own_half(rows):
    count = rows.shape[0] // 2
    return jnp.where(lax.axis_index("space") == 0, rows[:count], rows[count:])


def attend(half, blocks, query_ref, keys_ref, values_ref, weights_ref):
    rows = query_ref.shape[0]
    local_width = query_ref.shape[1]
    head_count = local_width // HEAD
    kept = slice(0, rows)
    if half is not None:
        rows = rows // 2
        kept = pl.ds(pl.multiple_of(half * rows, rows), rows)
    query = query_ref[kept, :]
    head_of = iota((rows, local_width), 1) // HEAD
    asked = [jnp.where(head_of == head, query, 0.0).astype(BF16) for head in range(head_count)]
    scores = rows_by(jnp.concatenate(asked, 0), keys_ref[kept, :]) * (1.0 / math.sqrt(HEAD))
    row, column = iota(scores.shape, 0) % rows, iota(scores.shape, 1)
    near = (row // blocks == column // blocks) & (jnp.abs(row - column) <= REACH)
    scores = jnp.where(near, scores, -1e30)
    raised = jnp.exp(scores - jnp.max(scores, -1, keepdims=True))
    shares = (raised / jnp.sum(raised, -1, keepdims=True)).astype(BF16)
    mixed = product(shares, values_ref[kept, :])
    total = mixed[0:rows]
    for head in range(1, head_count):
        total = jnp.where(head_of == head, mixed[head * rows : (head + 1) * rows], total)
    return product(total.astype(BF16), weights_ref[3]).astype(BF16)


def temporal_kernel(share, halved, term_count, own_ref, mods_ref, embed_ref, weights_ref, *refs):
    terms, (stream_ref, term_ref, query_ref, keys_ref, values_ref) = (
        refs[:term_count],
        refs[term_count:],
    )
    blocks = mods_ref.shape[0] // PIECES
    stream = product(own_ref[...].astype(BF16), embed_ref[...])
    stream = stream + piece_of(mods_ref, 2, share) * summed(terms)
    stream_ref[...] = own_half(stream) if halved else stream
    normed = layer_norm(stream) * (1.0 + piece_of(mods_ref, 4, share)) + piece_of(mods_ref, 3, share)
    normed = normed.astype(BF16)
    for ref, through in zip((query_ref, keys_ref, values_ref), projected(normed, weights_ref)):
        ref[...] = through.astype(BF16)
    half = 1 - lax.axis_index("space") if halved else None
    term_ref[...] = attend(half, blocks, query_ref, keys_ref, values_ref, weights_ref)


def kept_kernel(blocks, query_ref, keys_ref, values_ref, weights_ref, term_ref):
    half = lax.axis_index("space")
    term_ref[...] = attend(half, blocks, query_ref, keys_ref, values_ref, weights_ref)


def side_by_side(rows, blocks, share):
    parts = [rows[position * blocks : (position + 1) * blocks] for position in range(share)]
    return jnp.concatenate(parts + [jnp.zeros((blocks, LANES - share * CH), rows.dtype)], 1)


def final_kernel(share, halved, term_count, own_ref, stream_ref, mods_ref, final_ref, sizes_ref, *refs):
    terms, refs = refs[:term_count], refs[term_count:]
    blocks = mods_ref.shape[0] // PIECES
    rows = share * blocks
    own = own_half(own_ref[...]) if halved else own_ref[...]
    stream = stream_ref[...] + piece_of(mods_ref, 5, share) * summed(terms)
    velocity = rows_by(layer_norm(stream).astype(BF16), final_ref[...])
    sizes = jnp.concatenate([sizes_ref[:, :CH]] * share, 0)
    updated = own + sizes * velocity
    moved = jnp.concatenate([updated[1:], updated[:1]], 0)
    return blocks, rows, velocity, moved, refs


def between_kernel(share, term_count, iteration, noise_count, *refs):
    blocks, rows, velocity, moved, refs = final_kernel(share, False, term_count, *refs)
    noises, (cov_ref, velocity_ref, next_ref, sent_ref, noise_ref) = (
        refs[:noise_count],
        refs[noise_count:],
    )
    velocity_ref[...] = velocity
    devices = lax.axis_size("queue")
    here = lax.axis_index("queue")
    if noise_count == 2:
        mine, theirs = noises[0][iteration], noises[1][iteration]
        first = lax.axis_index("space") == 0
        noise = jnp.concatenate(
            [jnp.where(first, mine, theirs), jnp.where(first, theirs, mine)], 1
        )
    else:
        noise = noises[0][iteration]
    noise_ref[...] = noise.T
    next_ref[...] = moved
    for position in range(share):
        next_ref[(position + 1) * blocks - 1 : (position + 1) * blocks, :] = noise_ref[
            pl.ds(position * devices + here, 1), :
        ]
    hat = side_by_side(scaled(next_ref[...], cov_ref[...]), blocks, share)
    hat = jnp.where(iota((blocks, LANES), 1) == share * CH, 1.0, hat)
    sent_ref[...] = jnp.broadcast_to(hat.astype(BF16), sent_ref.shape)


def ending_kernel(share, halved, term_count, *refs):
    blocks, rows, velocity, moved, refs = final_kernel(share, halved, term_count, *refs)
    *earlier, sent_ref = refs
    pick = own_half if halved else lambda rows: rows
    sent_ref[...] = jnp.zeros_like(sent_ref)
    for at, values in enumerate([pick(ref[...]) for ref in earlier] + [velocity, moved]):
        wide = side_by_side(values, blocks, share)
        sent_ref[:, at : at + 1, :] = wide.reshape(blocks, 1, LANES)


def finish_kernel(share, arrived_ref, noise_ref, queue_ref, velocities_ref):
    devices = arrived_ref.shape[0]
    outs = []
    for at in range(STEPS + 1):
        turned = arrived_ref[:, at : at + 1, :].reshape(devices, LANES).T
        parts = [turned[position * CH : (position + 1) * CH] for position in range(share)]
        outs.append(jnp.concatenate(parts, 1))
    for step in range(STEPS):
        velocities_ref[step, 0] = outs[step]
    last = lax.axis_index("queue") == devices - 1
    queue_ref[0] = jnp.where(last, noise_ref[STEPS - 1], outs[STEPS])


def small(limit):
    return pltpu.CompilerParams(vmem_limit_bytes=limit * MIB)


def in_hbm(operands):
    return [pltpu.with_memory_space_constraint(operand, pltpu.HBM) for operand in operands]


def load(weights, first, count):
    shape = (count,) + weights.shape[1:]
    return pl.pallas_call(
        functools.partial(loader_kernel, first),
        out_shape=pltpu.VMEM(shape, weights.dtype),
        in_specs=[pl.BlockSpec(memory_space=pltpu.HBM)],
        out_specs=pl.BlockSpec(memory_space=pltpu.VMEM),
        scratch_shapes=[pltpu.SemaphoreType.DMA((count,))],
        compiler_params=small(1),
        cost_estimate=pl.CostEstimate(
            flops=0, bytes_accessed=2 * math.prod(shape), transcendentals=0
        ),
    )(*in_hbm([weights]))


def call(kernel, outs, operands, scratch=(), limit=8, held=True, from_hbm=()):
    specs = [pl.BlockSpec(memory_space=pltpu.VMEM)] * len(operands)
    specs += [pl.BlockSpec(memory_space=pltpu.HBM)] * len(from_hbm)
    if held:
        operands = [pltpu.with_memory_space_constraint(operand, pltpu.VMEM) for operand in operands]
    place = pltpu.VMEM if held else jax.ShapeDtypeStruct
    return pl.pallas_call(
        kernel,
        out_shape=[place(shape, dtype) for shape, dtype in outs],
        in_specs=specs,
        out_specs=[pl.BlockSpec(memory_space=pltpu.VMEM)] * len(outs),
        scratch_shapes=list(scratch),
        compiler_params=small(limit),
    )(*operands, *in_hbm(from_hbm))


def local(
    latents, fresh_noise, levels, modulation_weight, embed_weight, attention_weights, final_weight
):
    devices = lax.axis_size("queue")
    space_count = lax.axis_size("space")
    blocks = devices
    width = embed_weight.shape[1]
    local_width = attention_weights.shape[1]
    head_count = local_width // HEAD
    shard = latents.shape[1]
    tokens = shard * space_count
    share = tokens // devices
    rows = share * blocks
    wide_rows = share * CH + SLOTS
    run = functools.partial(call, limit=12 if rows <= 128 else 40)
    final_rows = final_weight.T
    latents = jnp.swapaxes(latents, 1, 2)
    fresh_noise = jnp.swapaxes(fresh_noise, 1, 2)

    def over_space(x):
        if space_count == 2:
            return [x, lax.ppermute(x, "space", [(0, 1), (1, 0)])]
        gathered = lax.all_gather(x, "space", axis=0, tiled=False)
        return [jnp.sum(gathered.astype(F32), 0)]

    def apart(x, mask):
        count = devices * space_count
        return lax.ppermute(x, ("queue", "space"), [(i, i ^ mask) for i in range(count)])

    def joined(*parts):
        shape = (len(parts) * parts[0].shape[0],) + parts[0].shape[1:]
        return run(join_kernel, [(shape, parts[0].dtype)], list(parts))[0]

    def after(x, *others):
        return lax.optimization_barrier((x, *others))[0]

    def basis(vectors, held):
        return run(
            functools.partial(basis_kernel, len(vectors)),
            [
                ((PIECES * blocks, width), F32),
                ((CH, CH), F32),
                ((3, blocks * CH, local_width), BF16),
                ((3, blocks, local_width), F32),
            ],
            [*vectors, embed_weight, held],
        )

    def forms(seen):
        return run(
            forms_kernel,
            [
                ((blocks, head_count * SLOTS, wide_rows), BF16),
                ((blocks, wide_rows, local_width), BF16),
            ],
            list(seen),
        )

    paired = space_count == 2 and devices == 16
    if paired:
        operands = (levels, modulation_weight, latents, embed_weight)
        vectors, sizes, packed, embed_weight = run(
            opening_kernel,
            [
                ((blocks, modulation_weight.shape[1]), BF16),
                ((blocks, LANES), F32),
                ((1, CH // 2, LANES), F32),
                (embed_weight.shape, BF16),
            ],
            [],
            [
                pltpu.SMEM(levels.shape, levels.dtype),
                pltpu.VMEM(modulation_weight.shape, modulation_weight.dtype),
                pltpu.VMEM(latents.shape, latents.dtype),
                pltpu.SemaphoreType.DMA((len(operands),)),
            ],
            from_hbm=operands,
        )
        vectors = over_space(vectors)
        spatial_weights = load(after(attention_weights, packed), 0, 4)
        arrivals = [apart(packed, mask) for mask in range(1, 8)]
        arrivals[-1] = after(arrivals[-1], spatial_weights)
        gathered = joined(packed, *arrivals)
        arrivals = [apart(gathered, mask) for mask in (8, 16, 24)]
        mods, cov, *seen = basis(vectors, spatial_weights)
        scores, values = forms(seen)
        arrivals[-1] = after(arrivals[-1], scores)
        gathered = [joined(gathered, *arrivals)]
    else:
        below = jnp.concatenate([jnp.zeros((1,), levels.dtype), levels[:-1]])
        sizes = jnp.broadcast_to(((below - levels).astype(F32) / LEVELS)[:, None], (blocks, LANES))
        part = product(time_features(levels), modulation_weight)
        part = lax.all_gather(part, "space", axis=1, tiled=True).reshape(blocks, PIECES, width)
        vectors = [jnp.swapaxes(part, 0, 1).reshape(PIECES * blocks, width)]
        gap = jnp.zeros((CH // 2, LANES // 2 - shard), F32)
        packed = jnp.concatenate([latents[0, : CH // 2], gap, latents[0, CH // 2 :], gap], 1)
        noises = [lax.all_gather(fresh_noise, "space", axis=2, tiled=True)]
        gathered = lax.all_gather(packed, ("queue", "space"), axis=0, tiled=False)
        gathered = [gathered.reshape(devices * space_count, CH // 2, LANES)]
        spatial_weights = load(attention_weights, 0, 4)
        mods, cov, *seen = basis(vectors, spatial_weights)
        scores, values = forms(seen)
    temporal_weights = None
    own = None
    velocities = []
    for iteration in range(STEPS):
        first = iteration == 0
        outs = [((rows, width), BF16)]
        scratch = [
            pltpu.VMEM((blocks * 8, local_width), F32),
            pltpu.VMEM((blocks * 8, head_count * SLOTS), F32),
            pltpu.VMEM((blocks, wide_rows, tokens) if first else (blocks, tokens, LANES), BF16),
        ]
        if first:
            outs.append(((rows, CH), F32))
            scratch.append(pltpu.VMEM((blocks, tokens, CH), F32))
        spatial_term, *new = run(
            functools.partial(spatial_kernel, first, paired, share),
            outs,
            [*gathered, *([] if first else [own]), cov, scores, values, spatial_weights],
            scratch,
        )
        if first:
            (own,) = new
            held, noise, spatial_term = lax.optimization_barrier(
                (attention_weights, fresh_noise, spatial_term)
            )
            temporal_weights = load(held, 4, 4)
            if paired:
                noises = over_space(noise)
        spatial_terms = over_space(spatial_term)
        if first and paired:
            spatial_terms[-1] = after(spatial_terms[-1], noises[-1])
        last = iteration == STEPS - 1
        halved = last and paired
        held_rows = rows // 2 if halved else rows
        asked = [((rows, local_width), BF16)] * 3
        stream, temporal_term, *asked = run(
            functools.partial(temporal_kernel, share, halved, len(spatial_terms)),
            [((held_rows, width), F32), ((held_rows, width), BF16)] + (asked if halved else []),
            [own, mods, embed_weight, temporal_weights, *spatial_terms],
            [] if halved else [pltpu.VMEM(shape, dtype) for shape, dtype in asked],
        )
        temporal_terms = over_space(temporal_term)
        if halved:
            temporal_terms[:1] = run(
                functools.partial(kept_kernel, blocks),
                [((held_rows, width), BF16)],
                [*asked, temporal_weights],
            )
        operands = [own, stream, mods, final_rows, sizes, *temporal_terms]
        if not last:
            velocity, own, sent = run(
                functools.partial(
                    between_kernel, share, len(temporal_terms), iteration, len(noises)
                ),
                [
                    ((rows, CH), F32),
                    ((rows, CH), F32),
                    ((devices if paired else 1, blocks, LANES), BF16),
                ],
                operands + [*noises, cov],
                [pltpu.VMEM((tokens, CH), F32)],
            )
            velocities.append(velocity)
            if paired:
                gathered = [lax.all_to_all(sent, "queue", 0, 0, tiled=True)]
            else:
                gathered = lax.all_gather(sent[0], "queue", axis=0, tiled=False)
                gathered = [jnp.swapaxes(gathered, 0, 1).reshape(devices * blocks, LANES)]
        else:
            (sent,) = run(
                functools.partial(
                    ending_kernel, share // 2 if halved else share, halved, len(temporal_terms)
                ),
                [((blocks, 8, LANES), F32)],
                operands + velocities,
            )
    arrived = lax.all_to_all(sent, "queue", 0, 0, tiled=True)
    if paired:
        queue_out, velocity_out = run(
            functools.partial(finish_kernel, share // 2),
            [((1, CH, shard), F32), ((STEPS, 1, CH, shard), F32)],
            [arrived, fresh_noise],
            held=False,
        )
    else:
        arrived = arrived[:, : STEPS + 1, : share * CH].reshape(devices, STEPS + 1, share, CH)
        arrived = arrived.transpose(1, 3, 2, 0).reshape(STEPS + 1, CH, tokens)
        arrived = lax.dynamic_slice_in_dim(arrived, lax.axis_index("space") * shard, shard, 2)
        velocity_out = arrived[:STEPS, None]
        last = lax.axis_index("queue") == devices - 1
        queue_out = jnp.where(last, fresh_noise[STEPS - 1], arrived[STEPS])[None]
    return jnp.swapaxes(queue_out, 1, 2), jnp.swapaxes(velocity_out, 2, 3)


def solution(mesh):
    in_specs = (
        P("queue", "space", None),
        P(None, "space", None),
        P(),
        P(None, "space"),
        P(),
        P(None, "space", None),
        P(),
    )
    out_specs = (P("queue", "space", None), P(None, "queue", "space", None))
    return jax.shard_map(local, mesh=mesh, in_specs=in_specs, out_specs=out_specs, check_vma=False)
```

```python
import functools
import math

import jax
import jax.numpy as jnp
from jax import lax
from jax.experimental import pallas as pl
from jax.experimental.pallas import tpu as pltpu
from jax.sharding import PartitionSpec as P

HEAD = 72
FREQ = 256
STEPS = 2
REACH = 4
LEVELS = 1000
CH = 16
PIECES = 6
LANES = 128
SLOTS = 32
GROUP = 16
MIB = 1024 * 1024
F32 = jnp.float32
BF16 = jnp.bfloat16
EXACT = lax.Precision.HIGHEST


def time_features(level_values):
    times = level_values.astype(F32) / LEVELS
    half_size = FREQ // 2
    frequency = jnp.exp(-math.log(10000.0) * jnp.arange(half_size).astype(F32) / half_size)
    angles = (times * 1000.0)[:, None] * frequency[None, :]
    return jnp.concatenate([jnp.cos(angles), jnp.sin(angles)], -1).astype(BF16)


def layer_norm(values):
    average = jnp.mean(values, -1, keepdims=True)
    centred = values - average
    variance = jnp.mean(centred * centred, -1, keepdims=True)
    return centred * lax.rsqrt(variance + 1e-06)


def iota(shape, dimension):
    return lax.broadcasted_iota(jnp.int32, shape, dimension)


def ones_where(condition, dtype=BF16):
    return jnp.where(condition, 1.0, 0.0).astype(dtype)


def rows_by(left, right, precision=None):
    return lax.dot_general(
        left, right, (((1,), (1,)), ((), ())), precision=precision, preferred_element_type=F32
    )


def product(left, right, precision=None):
    return jnp.dot(left, right, precision=precision, preferred_element_type=F32)


def projected(rows, weights_ref):
    local_width, width = weights_ref.shape[1:]
    through = rows_by(rows, weights_ref[0:3].reshape(3 * local_width, width))
    return [through[:, at * local_width : (at + 1) * local_width] for at in range(3)]


def over(count, body):
    if count <= 16:
        for at in range(count):
            body(at)
    else:
        lax.fori_loop(0, count, lambda at, _: body(at), None)


def rows_at(at, size):
    if isinstance(at, int):
        return slice(at * size, (at + 1) * size)
    return pl.ds(pl.multiple_of(at * size, size), size)


def piece_of(mods_ref, piece, share):
    blocks = mods_ref.shape[0] // PIECES
    return jnp.concatenate([mods_ref[piece * blocks : (piece + 1) * blocks, :]] * share, 0)


def scaled(latents, cov):
    x = latents.astype(BF16).astype(F32)
    variance = jnp.sum(x * product(x, cov, EXACT), -1, keepdims=True)
    return x * lax.rsqrt(jnp.maximum(variance, 0.0) + 1e-06)


def loader_kernel(first, weights_ref, held_ref, semaphores):
    copies = [
        pltpu.make_async_copy(weights_ref.at[first + at], held_ref.at[at], semaphores.at[at])
        for at in range(held_ref.shape[0])
    ]
    for copy in copies:
        copy.start()
    for copy in copies:
        copy.wait()


def pack_kernel(latents_hbm, packed_ref, latents_ref, semaphore):
    copy = pltpu.make_async_copy(latents_hbm, latents_ref, semaphore)
    copy.start()
    copy.wait()
    shard = latents_ref.shape[2]
    gap = jnp.zeros((CH // 2, LANES // 2 - shard), F32)
    packed = [latents_ref[0, : CH // 2], gap, latents_ref[0, CH // 2 :], gap]
    packed_ref[0] = jnp.concatenate(packed, 1)


def opening_kernel(
    levels_hbm, weight_hbm, embed_hbm, vectors_ref, sizes_ref, embed_ref,
    levels_ref, weight_ref, semaphores,
):
    pairs = ((levels_hbm, levels_ref), (weight_hbm, weight_ref), (embed_hbm, embed_ref))
    copies = [
        pltpu.make_async_copy(source, target, semaphores.at[at])
        for at, (source, target) in enumerate(pairs)
    ]
    for copy in copies:
        copy.start()
    copies[0].wait()
    blocks = vectors_ref.shape[0]
    shape = (blocks, FREQ // 2)
    frequency = jnp.exp(-math.log(10000.0) * iota(shape, 1).astype(F32) / (FREQ // 2))
    row = iota(shape, 0)
    level = jnp.zeros(shape, jnp.int32)
    below = jnp.zeros(shape, jnp.int32)
    for block in range(blocks):
        level = jnp.where(row == block, levels_ref[block], level)
        if block:
            below = jnp.where(row == block, levels_ref[block - 1], below)
    sizes_ref[...] = (below - level).astype(F32) / LEVELS
    angles = (level.astype(F32) / LEVELS * 1000.0) * frequency
    features = jnp.concatenate([jnp.cos(angles), jnp.sin(angles)], -1).astype(BF16)
    copies[1].wait()
    vectors_ref[...] = product(features, weight_ref[...]).astype(BF16)
    copies[2].wait()


def join_kernel(*refs):
    *parts, joined_ref = refs
    count = parts[0].shape[0]
    for at, part in enumerate(parts):
        joined_ref[at * count : (at + 1) * count] = part[...]


def basis_kernel(sources, *refs):
    vectors, refs = refs[:sources], refs[sources:]
    embed_ref, weights_ref, mods_ref, cov_ref, rows_ref, last_ref = refs
    blocks = last_ref.shape[1]
    width = weights_ref.shape[2]
    if sources == 2:
        first = lax.axis_index("space") == 0
        mine, theirs = vectors[0][...].astype(F32), vectors[1][...].astype(F32)
        lower = jnp.where(first, mine, theirs)
        upper = jnp.where(first, theirs, mine)
        for piece in range(PIECES):
            part = (lower if piece < 3 else upper)[:, piece % 3 * width : (piece % 3 + 1) * width]
            mods_ref[piece * blocks : (piece + 1) * blocks, :] = part
    else:
        mods_ref[...] = vectors[0][...]
    embed = embed_ref[...].astype(F32)
    centred = embed - jnp.mean(embed, -1, keepdims=True)
    cov_ref[...] = rows_by(centred, centred, EXACT) / width
    scale = 1.0 + mods_ref[blocks : 2 * blocks, :]
    spread = [(centred * scale[block : block + 1, :]).astype(BF16) for block in range(blocks)]
    spread = jnp.concatenate(spread + [mods_ref[0:blocks, :].astype(BF16)], 0)
    for matrix, through in enumerate(projected(spread, weights_ref)):
        rows_ref[matrix] = through[: blocks * CH].astype(BF16)
        last_ref[matrix] = through[blocks * CH :]


def forms_kernel(rows_ref, last_ref, scores_ref, values_ref):
    blocks = scores_ref.shape[0]
    local_width = rows_ref.shape[2]
    share = (LANES - SLOTS) // CH
    head_count = local_width // HEAD
    head_mask = iota((head_count * SLOTS, local_width), 0) // SLOTS == (
        iota((head_count * SLOTS, local_width), 1) // HEAD
    )

    def per_block(block):
        def constant(matrix, size):
            row = last_ref[matrix, pl.ds(block, 1), :]
            return jnp.where(iota((size, local_width), 0) == 0, row, 0.0).astype(BF16)

        def tiled(matrix):
            rows = rows_ref[matrix, rows_at(block, CH), :]
            return jnp.concatenate([rows] * share + [constant(matrix, SLOTS)], 0)

        query = jnp.concatenate([rows_ref[0, rows_at(block, CH), :], constant(0, SLOTS - CH)], 0)
        query = jnp.where(head_mask, jnp.concatenate([query] * head_count, 0), 0.0).astype(BF16)
        scores_ref[block] = rows_by(query, tiled(1)).astype(BF16)
        values_ref[block] = tiled(2)

    over(blocks, per_block)


def spatial_kernel(first, turned, share, *refs):
    if first:
        gathered_ref, cov_ref, scores_ref, values_ref, weights_ref, *refs = refs
    else:
        gathered_ref, own_ref, cov_ref, scores_ref, values_ref, weights_ref, *refs = refs
    if first:
        term_ref, own_ref, attended_ref, asked_ref, keys_ref, natural_ref = refs
    else:
        term_ref, attended_ref, asked_ref, keys_ref = refs
    blocks = scores_ref.shape[0]
    local_width = values_ref.shape[2]
    head_count = local_width // HEAD
    devices = lax.axis_size("queue")
    tokens = share * devices
    here = lax.axis_index("queue")
    cov = cov_ref[...]

    if first:
        parts = gathered_ref.shape[0] // blocks
        shard = tokens // parts
        base = here * parts + lax.axis_index("space") if turned else 0
        filling = jnp.zeros((share * CH - CH, tokens), BF16)
        constant = ones_where(iota((SLOTS, tokens), 0) == 0)

        def keys_of(block):
            pieces = [
                gathered_ref[jnp.bitwise_xor(base, block * parts + part)] for part in range(parts)
            ]
            top = jnp.concatenate([piece[:, :shard] for piece in pieces], 1)
            low = jnp.concatenate(
                [piece[:, LANES // 2 : LANES // 2 + shard] for piece in pieces], 1
            )
            raw = jnp.concatenate([top, low], 0)
            natural_ref[block] = raw.T
            x = raw.astype(BF16).astype(F32)
            variance = jnp.sum(x * product(cov, x, EXACT), 0, keepdims=True)
            hat = x * lax.rsqrt(jnp.maximum(variance, 0.0) + 1e-06)
            keys_ref[block] = jnp.concatenate([hat.astype(BF16), filling, constant], 0)

        over(blocks, keys_of)

        def own_of(block):
            for position in range(share):
                own_ref[pl.ds(position * blocks + block, 1), :] = natural_ref[
                    block, pl.ds(position * devices + here, 1), :
                ]

        over(blocks, own_of)
    else:
        lane = iota((devices, LANES), 1) // CH
        held = gathered_ref[...].reshape(devices * blocks, LANES)
        if turned:
            row, column = iota((devices * blocks,) * 2, 0), iota((devices * blocks,) * 2, 1)
            moved = ones_where(column == row % devices * blocks + row // devices)
            held = product(moved, held).astype(BF16)
        natural = held.reshape(blocks, devices, LANES)
        for block in range(blocks):
            keys_ref[block] = jnp.concatenate(
                [
                    jnp.where((lane == position) | (lane == share), natural[block], 0.0).astype(BF16)
                    for position in range(share)
                ],
                0,
            )

    rows = share * blocks
    hat = scaled(own_ref[...], cov).astype(BF16)
    lanes = head_count * SLOTS
    wide = product(hat, ones_where(iota((CH, lanes), 1) % SLOTS == iota((CH, lanes), 0)))
    wide = jnp.where(iota((rows, lanes), 1) % SLOTS == CH, 1.0, wide).astype(BF16)
    row, column = iota((blocks * 8, rows), 0), iota((blocks * 8, rows), 1)
    moved = ones_where((row % 8 == column // blocks) & (row // 8 == column % blocks))
    asked_ref[...] = product(moved, wide)
    asked_mask = iota((head_count * 8, lanes), 0) // 8 == iota((head_count * 8, lanes), 1) // SLOTS
    head_of = iota((8, local_width), 1) // HEAD

    def asked_of(block):
        asked = jnp.concatenate([asked_ref[rows_at(block, 8), :]] * head_count, 0)
        return jnp.where(asked_mask, asked, 0.0).astype(BF16)

    def softmax(scores):
        scores = scores * (1.0 / math.sqrt(HEAD))
        raised = jnp.exp(scores - jnp.max(scores, -1, keepdims=True))
        return (raised / jnp.sum(raised, -1, keepdims=True)).astype(BF16)

    def attend(group):
        members = [group * GROUP + at for at in range(GROUP)]
        queries = [product(asked_of(block), scores_ref[block]).astype(BF16) for block in members]
        meet = product if first else rows_by
        scores = [meet(query, keys_ref[block]) for query, block in zip(queries, members)]
        shares = [softmax(score) for score in scores]
        mix = rows_by if first else product
        mixed = [mix(part, keys_ref[block]).astype(BF16) for part, block in zip(shares, members)]
        mixed = [product(part, values_ref[block]) for part, block in zip(mixed, members)]
        for part, block in zip(mixed, members):
            total = part[0:8]
            for head in range(1, head_count):
                total = jnp.where(head_of == head, part[head * 8 : (head + 1) * 8], total)
            attended_ref[rows_at(block, 8), :] = total

    over(blocks // GROUP, attend)
    row, column = iota((rows, blocks * 8), 0), iota((rows, blocks * 8), 1)
    moved = ones_where((row // blocks == column % 8) & (row % blocks == column // 8))
    attended = product(moved, attended_ref[...].astype(BF16)).astype(BF16)
    term_ref[...] = product(attended, weights_ref[3]).astype(BF16)


def summed(terms):
    total = terms[0][...].astype(F32)
    for term in terms[1:]:
        total = total + term[...].astype(F32)
    return total


def own_half(rows):
    count = rows.shape[0] // 2
    return jnp.where(lax.axis_index("space") == 0, rows[:count], rows[count:])


def attend(half, blocks, query_ref, keys_ref, values_ref, weights_ref):
    rows = query_ref.shape[0]
    local_width = query_ref.shape[1]
    head_count = local_width // HEAD
    kept = slice(0, rows)
    if half is not None:
        rows = rows // 2
        kept = pl.ds(pl.multiple_of(half * rows, rows), rows)
    query = query_ref[kept, :]
    head_of = iota((rows, local_width), 1) // HEAD
    asked = [jnp.where(head_of == head, query, 0.0).astype(BF16) for head in range(head_count)]
    scores = rows_by(jnp.concatenate(asked, 0), keys_ref[kept, :]) * (1.0 / math.sqrt(HEAD))
    row, column = iota(scores.shape, 0) % rows, iota(scores.shape, 1)
    near = (row // blocks == column // blocks) & (jnp.abs(row - column) <= REACH)
    scores = jnp.where(near, scores, -1e30)
    raised = jnp.exp(scores - jnp.max(scores, -1, keepdims=True))
    shares = (raised / jnp.sum(raised, -1, keepdims=True)).astype(BF16)
    mixed = product(shares, values_ref[kept, :])
    total = mixed[0:rows]
    for head in range(1, head_count):
        total = jnp.where(head_of == head, mixed[head * rows : (head + 1) * rows], total)
    return product(total.astype(BF16), weights_ref[3]).astype(BF16)


def temporal_kernel(share, halved, term_count, own_ref, mods_ref, embed_ref, weights_ref, *refs):
    terms, (stream_ref, term_ref, query_ref, keys_ref, values_ref) = (
        refs[:term_count],
        refs[term_count:],
    )
    blocks = mods_ref.shape[0] // PIECES
    stream = product(own_ref[...].astype(BF16), embed_ref[...])
    stream = stream + piece_of(mods_ref, 2, share) * summed(terms)
    stream_ref[...] = own_half(stream) if halved else stream
    normed = layer_norm(stream) * (1.0 + piece_of(mods_ref, 4, share)) + piece_of(mods_ref, 3, share)
    normed = normed.astype(BF16)
    if halved:
        parts = [rows_by(normed, weights_ref[matrix]) for matrix in range(3)]
    else:
        parts = projected(normed, weights_ref)
    for ref, part in zip((query_ref, keys_ref, values_ref), parts):
        ref[...] = part.astype(BF16)
    half = 1 - lax.axis_index("space") if halved else None
    term_ref[...] = attend(half, blocks, query_ref, keys_ref, values_ref, weights_ref)


def kept_kernel(blocks, query_ref, keys_ref, values_ref, weights_ref, term_ref):
    half = lax.axis_index("space")
    term_ref[...] = attend(half, blocks, query_ref, keys_ref, values_ref, weights_ref)


def side_by_side(rows, blocks, share):
    parts = [rows[position * blocks : (position + 1) * blocks] for position in range(share)]
    return jnp.concatenate(parts + [jnp.zeros((blocks, LANES - share * CH), rows.dtype)], 1)


def final_kernel(share, halved, term_count, own_ref, stream_ref, mods_ref, final_ref, sizes_ref, *refs):
    terms, refs = refs[:term_count], refs[term_count:]
    blocks = mods_ref.shape[0] // PIECES
    rows = share * blocks
    own = own_half(own_ref[...]) if halved else own_ref[...]
    stream = stream_ref[...] + piece_of(mods_ref, 5, share) * summed(terms)
    velocity = rows_by(layer_norm(stream).astype(BF16), final_ref[...])
    sizes = jnp.concatenate([sizes_ref[:, :CH]] * share, 0)
    updated = own + sizes * velocity
    moved = jnp.concatenate([updated[1:], updated[:1]], 0)
    return blocks, rows, velocity, moved, refs


def noise_kernel(share, iteration, *refs):
    *noises, rows_ref, noise_ref = refs
    devices = lax.axis_size("queue")
    here = lax.axis_index("queue")
    noise = noises[0][iteration]
    if len(noises) == 2:
        theirs = noises[1][iteration]
        first = lax.axis_index("space") == 0
        noise = jnp.concatenate(
            [jnp.where(first, noise, theirs), jnp.where(first, theirs, noise)], 1
        )
    noise_ref[...] = noise.T
    rows_ref[...] = jnp.zeros_like(rows_ref)
    for position in range(share):
        rows_ref[position : position + 1, :] = noise_ref[pl.ds(position * devices + here, 1), :]


def between_kernel(share, term_count, *refs):
    blocks, rows, velocity, moved, refs = final_kernel(share, False, term_count, *refs)
    noise_ref, cov_ref, velocity_ref, next_ref, sent_ref = refs
    velocity_ref[...] = velocity
    next_ref[...] = moved
    for position in range(share):
        next_ref[(position + 1) * blocks - 1 : (position + 1) * blocks, :] = noise_ref[
            position : position + 1, :
        ]
    hat = side_by_side(scaled(next_ref[...], cov_ref[...]), blocks, share)
    hat = jnp.where(iota((blocks, LANES), 1) == share * CH, 1.0, hat)
    sent_ref[...] = jnp.broadcast_to(hat.astype(BF16), sent_ref.shape)


def ending_kernel(share, halved, term_count, *refs):
    blocks, rows, velocity, moved, refs = final_kernel(share, halved, term_count, *refs)
    *earlier, sent_ref = refs
    pick = own_half if halved else lambda rows: rows
    sent_ref[...] = jnp.zeros_like(sent_ref)
    for at, values in enumerate([pick(ref[...]) for ref in earlier] + [velocity, moved]):
        wide = side_by_side(values, blocks, share)
        sent_ref[:, at : at + 1, :] = wide.reshape(blocks, 1, LANES)


def finish_kernel(share, arrived_ref, noise_ref, queue_ref, velocities_ref):
    devices = arrived_ref.shape[0]
    outs = []
    for at in range(STEPS + 1):
        turned = arrived_ref[:, at : at + 1, :].reshape(devices, LANES).T
        parts = [turned[position * CH : (position + 1) * CH] for position in range(share)]
        outs.append(jnp.concatenate(parts, 1))
    for step in range(STEPS):
        velocities_ref[step, 0] = outs[step]
    last = lax.axis_index("queue") == devices - 1
    queue_ref[0] = jnp.where(last, noise_ref[STEPS - 1], outs[STEPS])


def small(limit):
    return pltpu.CompilerParams(vmem_limit_bytes=limit * MIB)


def in_hbm(operands):
    return [pltpu.with_memory_space_constraint(operand, pltpu.HBM) for operand in operands]


def load(weights, first, count):
    shape = (count,) + weights.shape[1:]
    return pl.pallas_call(
        functools.partial(loader_kernel, first),
        out_shape=pltpu.VMEM(shape, weights.dtype),
        in_specs=[pl.BlockSpec(memory_space=pltpu.HBM)],
        out_specs=pl.BlockSpec(memory_space=pltpu.VMEM),
        scratch_shapes=[pltpu.SemaphoreType.DMA((count,))],
        compiler_params=small(1),
        cost_estimate=pl.CostEstimate(
            flops=0, bytes_accessed=2 * math.prod(shape), transcendentals=0
        ),
    )(*in_hbm([weights]))


def call(kernel, outs, operands, scratch=(), limit=8, held=True, from_hbm=()):
    specs = [pl.BlockSpec(memory_space=pltpu.VMEM)] * len(operands)
    specs += [pl.BlockSpec(memory_space=pltpu.HBM)] * len(from_hbm)
    if held:
        operands = [pltpu.with_memory_space_constraint(operand, pltpu.VMEM) for operand in operands]
    place = pltpu.VMEM if held else jax.ShapeDtypeStruct
    return pl.pallas_call(
        kernel,
        out_shape=[place(shape, dtype) for shape, dtype in outs],
        in_specs=specs,
        out_specs=[pl.BlockSpec(memory_space=pltpu.VMEM)] * len(outs),
        scratch_shapes=list(scratch),
        compiler_params=small(limit),
    )(*operands, *in_hbm(from_hbm))


def local(
    latents, fresh_noise, levels, modulation_weight, embed_weight, attention_weights, final_weight
):
    devices = lax.axis_size("queue")
    space_count = lax.axis_size("space")
    blocks = devices
    width = embed_weight.shape[1]
    local_width = attention_weights.shape[1]
    head_count = local_width // HEAD
    shard = latents.shape[1]
    tokens = shard * space_count
    share = tokens // devices
    rows = share * blocks
    wide_rows = share * CH + SLOTS
    run = functools.partial(call, limit=12 if rows <= 128 else 40)
    final_rows = final_weight.T
    latents = jnp.swapaxes(latents, 1, 2)
    fresh_noise = jnp.swapaxes(fresh_noise, 1, 2)

    def over_space(x):
        if space_count == 2:
            return [x, lax.ppermute(x, "space", [(0, 1), (1, 0)])]
        gathered = lax.all_gather(x, "space", axis=0, tiled=False)
        return [jnp.sum(gathered.astype(F32), 0)]

    def apart(x, mask):
        count = devices * space_count
        return lax.ppermute(x, ("queue", "space"), [(i, i ^ mask) for i in range(count)])

    def joined(*parts):
        shape = (len(parts) * parts[0].shape[0],) + parts[0].shape[1:]
        return run(join_kernel, [(shape, parts[0].dtype)], list(parts))[0]

    def after(x, *others):
        return lax.optimization_barrier((x, *others))[0]

    def basis(vectors, held):
        return run(
            functools.partial(basis_kernel, len(vectors)),
            [
                ((PIECES * blocks, width), F32),
                ((CH, CH), F32),
                ((3, blocks * CH, local_width), BF16),
                ((3, blocks, local_width), F32),
            ],
            [*vectors, embed_weight, held],
        )

    def forms(seen):
        return run(
            forms_kernel,
            [
                ((blocks, head_count * SLOTS, wide_rows), BF16),
                ((blocks, wide_rows, local_width), BF16),
            ],
            list(seen),
        )

    paired = space_count == 2 and devices == 16
    if paired:
        (packed,) = run(
            pack_kernel,
            [((1, CH // 2, LANES), F32)],
            [],
            [pltpu.VMEM(latents.shape, latents.dtype), pltpu.SemaphoreType.DMA],
            from_hbm=[latents],
        )
        other = apart(packed, 1)
        operands = (after(levels, packed), modulation_weight, embed_weight)
        vectors, sizes, embed_weight = run(
            opening_kernel,
            [
                ((blocks, modulation_weight.shape[1]), BF16),
                ((blocks, LANES), F32),
                (embed_weight.shape, BF16),
            ],
            [],
            [
                pltpu.SMEM(levels.shape, levels.dtype),
                pltpu.VMEM(modulation_weight.shape, modulation_weight.dtype),
                pltpu.SemaphoreType.DMA((len(operands),)),
            ],
            from_hbm=operands,
        )
        gathered = joined(packed, after(other, vectors))
        vectors = over_space(after(vectors, gathered))
        arrivals = [apart(gathered, mask) for mask in (2, 4, 6)]
        spatial_weights = load(after(attention_weights, gathered), 0, 4)
        arrivals[-1] = after(arrivals[-1], spatial_weights)
        gathered = joined(gathered, *arrivals)
        arrivals = [apart(gathered, mask) for mask in (8, 16, 24)]
        mods, cov, *seen = basis(vectors, spatial_weights)
        scores, values = forms(seen)
        arrivals[-1] = after(arrivals[-1], scores)
        gathered = [joined(gathered, *arrivals)]
    else:
        below = jnp.concatenate([jnp.zeros((1,), levels.dtype), levels[:-1]])
        sizes = jnp.broadcast_to(((below - levels).astype(F32) / LEVELS)[:, None], (blocks, LANES))
        part = product(time_features(levels), modulation_weight)
        part = lax.all_gather(part, "space", axis=1, tiled=True).reshape(blocks, PIECES, width)
        vectors = [jnp.swapaxes(part, 0, 1).reshape(PIECES * blocks, width)]
        gap = jnp.zeros((CH // 2, LANES // 2 - shard), F32)
        packed = jnp.concatenate([latents[0, : CH // 2], gap, latents[0, CH // 2 :], gap], 1)
        noises = [lax.all_gather(fresh_noise, "space", axis=2, tiled=True)]
        gathered = lax.all_gather(packed, ("queue", "space"), axis=0, tiled=False)
        gathered = [gathered.reshape(devices * space_count, CH // 2, LANES)]
        spatial_weights = load(attention_weights, 0, 4)
        mods, cov, *seen = basis(vectors, spatial_weights)
        scores, values = forms(seen)
    temporal_weights = None
    own = None
    velocities = []
    for iteration in range(STEPS):
        first = iteration == 0
        outs = [((rows, width), BF16)]
        scratch = [
            pltpu.VMEM((blocks * 8, local_width), F32),
            pltpu.VMEM((blocks * 8, head_count * SLOTS), F32),
            pltpu.VMEM((blocks, wide_rows, tokens) if first else (blocks, tokens, LANES), BF16),
        ]
        if first:
            outs.append(((rows, CH), F32))
            scratch.append(pltpu.VMEM((blocks, tokens, CH), F32))
        spatial_term, *new = run(
            functools.partial(spatial_kernel, first, paired, share),
            outs,
            [*gathered, *([] if first else [own]), cov, scores, values, spatial_weights],
            scratch,
        )
        if first:
            (own,) = new
            held, noise, spatial_term = lax.optimization_barrier(
                (attention_weights, fresh_noise, spatial_term)
            )
            temporal_weights = load(held, 4, 4)
            if paired:
                noises = over_space(noise)
        spatial_terms = over_space(spatial_term)
        if first and paired:
            spatial_terms[-1] = after(spatial_terms[-1], noises[-1])
        last = iteration == STEPS - 1
        halved = last and paired
        held_rows = rows // 2 if halved else rows
        asked = [((rows, local_width), BF16)] * 3
        stream, temporal_term, *asked = run(
            functools.partial(temporal_kernel, share, halved, len(spatial_terms)),
            [((held_rows, width), F32), ((held_rows, width), BF16)] + (asked if halved else []),
            [own, mods, embed_weight, temporal_weights, *spatial_terms],
            [] if halved else [pltpu.VMEM(shape, dtype) for shape, dtype in asked],
        )
        temporal_terms = over_space(temporal_term)
        if halved:
            temporal_terms[:1] = run(
                functools.partial(kept_kernel, blocks),
                [((held_rows, width), BF16)],
                [*asked, temporal_weights],
            )
        if not last:
            noises[0] = after(noises[0], temporal_term)
            (noise,) = run(
                functools.partial(noise_kernel, share, iteration),
                [((8, CH), F32)],
                noises,
                [pltpu.VMEM((tokens, CH), F32)],
            )
            temporal_terms[-1] = after(temporal_terms[-1], noise)
        operands = [own, stream, mods, final_rows, sizes, *temporal_terms]
        if not last:
            velocity, own, sent = run(
                functools.partial(between_kernel, share, len(temporal_terms)),
                [
                    ((rows, CH), F32),
                    ((rows, CH), F32),
                    ((devices if paired else 1, blocks, LANES), BF16),
                ],
                operands + [noise, cov],
            )
            velocities.append(velocity)
            if paired:
                gathered = [lax.all_to_all(sent, "queue", 0, 0, tiled=True)]
            else:
                gathered = lax.all_gather(sent[0], "queue", axis=0, tiled=False)
                gathered = [jnp.swapaxes(gathered, 0, 1).reshape(devices * blocks, LANES)]
        else:
            (sent,) = run(
                functools.partial(
                    ending_kernel, share // 2 if halved else share, halved, len(temporal_terms)
                ),
                [((blocks, 8, LANES), F32)],
                operands + velocities,
            )
    arrived = lax.all_to_all(sent, "queue", 0, 0, tiled=True)
    if paired:
        queue_out, velocity_out = run(
            functools.partial(finish_kernel, share // 2),
            [((1, CH, shard), F32), ((STEPS, 1, CH, shard), F32)],
            [arrived, fresh_noise],
            held=False,
        )
    else:
        arrived = arrived[:, : STEPS + 1, : share * CH].reshape(devices, STEPS + 1, share, CH)
        arrived = arrived.transpose(1, 3, 2, 0).reshape(STEPS + 1, CH, tokens)
        arrived = lax.dynamic_slice_in_dim(arrived, lax.axis_index("space") * shard, shard, 2)
        velocity_out = arrived[:STEPS, None]
        last = lax.axis_index("queue") == devices - 1
        queue_out = jnp.where(last, fresh_noise[STEPS - 1], arrived[STEPS])[None]
    return jnp.swapaxes(queue_out, 1, 2), jnp.swapaxes(velocity_out, 2, 3)


def solution(mesh):
    in_specs = (
        P("queue", "space", None),
        P(None, "space", None),
        P(),
        P(None, "space"),
        P(),
        P(None, "space", None),
        P(),
    )
    out_specs = (P("queue", "space", None), P(None, "queue", "space", None))
    return jax.shard_map(local, mesh=mesh, in_specs=in_specs, out_specs=out_specs, check_vma=False)
```

```python
import functools
import math

import jax
import jax.numpy as jnp
from jax import lax
from jax.experimental import pallas as pl
from jax.experimental.pallas import tpu as pltpu
from jax.sharding import PartitionSpec as P

HEAD = 72
FREQ = 256
STEPS = 2
REACH = 4
LEVELS = 1000
CH = 16
PIECES = 6
LANES = 128
SLOTS = 32
GROUP = 16
BANDS = 4
MIB = 1024 * 1024
F32 = jnp.float32
BF16 = jnp.bfloat16
EXACT = lax.Precision.HIGHEST


def time_features(level_values):
    times = level_values.astype(F32) / LEVELS
    half_size = FREQ // 2
    frequency = jnp.exp(-math.log(10000.0) * jnp.arange(half_size).astype(F32) / half_size)
    angles = (times * 1000.0)[:, None] * frequency[None, :]
    return jnp.concatenate([jnp.cos(angles), jnp.sin(angles)], -1).astype(BF16)


def layer_norm(values):
    average = jnp.mean(values, -1, keepdims=True)
    centred = values - average
    variance = jnp.mean(centred * centred, -1, keepdims=True)
    return centred * lax.rsqrt(variance + 1e-06)


def iota(shape, dimension):
    return lax.broadcasted_iota(jnp.int32, shape, dimension)


def ones_where(condition, dtype=BF16):
    return jnp.where(condition, 1.0, 0.0).astype(dtype)


def rows_by(left, right, precision=None):
    return lax.dot_general(
        left, right, (((1,), (1,)), ((), ())), precision=precision, preferred_element_type=F32
    )


def product(left, right, precision=None):
    return jnp.dot(left, right, precision=precision, preferred_element_type=F32)


def projected(rows, weights_ref):
    local_width, width = weights_ref.shape[1:]
    through = rows_by(rows, weights_ref[0:3].reshape(3 * local_width, width))
    return [through[:, at * local_width : (at + 1) * local_width] for at in range(3)]


def over(count, body):
    if count <= 16:
        for at in range(count):
            body(at)
    else:
        lax.fori_loop(0, count, lambda at, _: body(at), None)


def rows_at(at, size):
    if isinstance(at, int):
        return slice(at * size, (at + 1) * size)
    return pl.ds(pl.multiple_of(at * size, size), size)


def piece_of(mods_ref, piece, share):
    blocks = mods_ref.shape[0] // PIECES
    return jnp.concatenate([mods_ref[piece * blocks : (piece + 1) * blocks, :]] * share, 0)


def scaled(latents, cov):
    x = latents.astype(BF16).astype(F32)
    variance = jnp.sum(x * product(x, cov, EXACT), -1, keepdims=True)
    return x * lax.rsqrt(jnp.maximum(variance, 0.0) + 1e-06)


def pieces_of(source, target):
    rows = target.shape[0]
    band = rows // BANDS if rows % (16 * BANDS) == 0 else rows
    return [
        (source.at[pl.ds(at, band), :], target.at[pl.ds(at, band), :])
        for at in range(0, rows, band)
    ]


def loader_kernel(first, weights_ref, held_ref, semaphores):
    pairs = [
        pair
        for at in range(held_ref.shape[0])
        for pair in pieces_of(weights_ref.at[first + at], held_ref.at[at])
    ]
    copies = [
        pltpu.make_async_copy(source, target, semaphores.at[at])
        for at, (source, target) in enumerate(pairs)
    ]
    for copy in copies:
        copy.start()
    for copy in copies:
        copy.wait()


def opening_kernel(
    levels_hbm, weight_hbm, latents_hbm, embed_hbm, vectors_ref, sizes_ref, packed_ref, embed_ref,
    levels_ref, weight_ref, latents_ref, semaphores,
):
    bands = pieces_of(weight_hbm, weight_ref)
    pairs = [(levels_hbm, levels_ref), (latents_hbm, latents_ref), *bands, (embed_hbm, embed_ref)]
    copies = [
        pltpu.make_async_copy(source, target, semaphores.at[at])
        for at, (source, target) in enumerate(pairs)
    ]
    for copy in copies:
        copy.start()
    copies[0].wait()
    blocks = vectors_ref.shape[0]
    shape = (blocks, FREQ // 2)
    frequency = jnp.exp(-math.log(10000.0) * iota(shape, 1).astype(F32) / (FREQ // 2))
    row = iota(shape, 0)
    level = jnp.zeros(shape, jnp.int32)
    below = jnp.zeros(shape, jnp.int32)
    for block in range(blocks):
        level = jnp.where(row == block, levels_ref[block], level)
        if block:
            below = jnp.where(row == block, levels_ref[block - 1], below)
    sizes_ref[...] = (below - level).astype(F32) / LEVELS
    angles = (level.astype(F32) / LEVELS * 1000.0) * frequency
    features = jnp.concatenate([jnp.cos(angles), jnp.sin(angles)], -1).astype(BF16)
    copies[1].wait()
    shard = latents_ref.shape[2]
    gap = jnp.zeros((CH // 2, LANES // 2 - shard), F32)
    packed = [latents_ref[0, : CH // 2], gap, latents_ref[0, CH // 2 :], gap]
    packed_ref[0] = jnp.concatenate(packed, 1)
    for copy in copies[2:]:
        copy.wait()
    vectors_ref[...] = product(features, weight_ref[...]).astype(BF16)


def join_kernel(*refs):
    *parts, joined_ref = refs
    count = parts[0].shape[0]
    for at, part in enumerate(parts):
        joined_ref[at * count : (at + 1) * count] = part[...]


def basis_kernel(sources, *refs):
    vectors, refs = refs[:sources], refs[sources:]
    embed_ref, weights_ref, mods_ref, cov_ref, rows_ref, last_ref = refs
    blocks = last_ref.shape[1]
    width = weights_ref.shape[2]
    if sources == 2:
        first = lax.axis_index("space") == 0
        mine, theirs = vectors[0][...].astype(F32), vectors[1][...].astype(F32)
        lower = jnp.where(first, mine, theirs)
        upper = jnp.where(first, theirs, mine)
        for piece in range(PIECES):
            part = (lower if piece < 3 else upper)[:, piece % 3 * width : (piece % 3 + 1) * width]
            mods_ref[piece * blocks : (piece + 1) * blocks, :] = part
    else:
        mods_ref[...] = vectors[0][...]
    embed = embed_ref[...].astype(F32)
    centred = embed - jnp.mean(embed, -1, keepdims=True)
    cov_ref[...] = rows_by(centred, centred, EXACT) / width
    scale = 1.0 + mods_ref[blocks : 2 * blocks, :]
    spread = [(centred * scale[block : block + 1, :]).astype(BF16) for block in range(blocks)]
    spread = jnp.concatenate(spread + [mods_ref[0:blocks, :].astype(BF16)], 0)
    for matrix, through in enumerate(projected(spread, weights_ref)):
        rows_ref[matrix] = through[: blocks * CH].astype(BF16)
        last_ref[matrix] = through[blocks * CH :]


def forms_kernel(rows_ref, last_ref, scores_ref, values_ref):
    blocks = scores_ref.shape[0]
    local_width = rows_ref.shape[2]
    share = (LANES - SLOTS) // CH
    head_count = local_width // HEAD
    head_mask = iota((head_count * SLOTS, local_width), 0) // SLOTS == (
        iota((head_count * SLOTS, local_width), 1) // HEAD
    )

    def per_block(block):
        def constant(matrix, size):
            row = last_ref[matrix, pl.ds(block, 1), :]
            return jnp.where(iota((size, local_width), 0) == 0, row, 0.0).astype(BF16)

        def tiled(matrix):
            rows = rows_ref[matrix, rows_at(block, CH), :]
            return jnp.concatenate([rows] * share + [constant(matrix, SLOTS)], 0)

        query = jnp.concatenate([rows_ref[0, rows_at(block, CH), :], constant(0, SLOTS - CH)], 0)
        query = jnp.where(head_mask, jnp.concatenate([query] * head_count, 0), 0.0).astype(BF16)
        scores_ref[block] = rows_by(query, tiled(1)).astype(BF16)
        values_ref[block] = tiled(2)

    over(blocks, per_block)


def spatial_kernel(first, turned, share, *refs):
    if first:
        gathered_ref, cov_ref, scores_ref, values_ref, weights_ref, *refs = refs
    else:
        gathered_ref, own_ref, cov_ref, scores_ref, values_ref, weights_ref, *refs = refs
    if first:
        term_ref, own_ref, attended_ref, asked_ref, keys_ref, natural_ref = refs
    else:
        term_ref, attended_ref, asked_ref, keys_ref = refs
    blocks = scores_ref.shape[0]
    local_width = values_ref.shape[2]
    head_count = local_width // HEAD
    devices = lax.axis_size("queue")
    tokens = share * devices
    here = lax.axis_index("queue")
    cov = cov_ref[...]

    if first:
        parts = gathered_ref.shape[0] // blocks
        shard = tokens // parts
        base = here * parts + lax.axis_index("space") if turned else 0
        filling = jnp.zeros((share * CH - CH, tokens), BF16)
        constant = ones_where(iota((SLOTS, tokens), 0) == 0)

        def keys_of(block):
            pieces = [
                gathered_ref[jnp.bitwise_xor(base, block * parts + part)] for part in range(parts)
            ]
            top = jnp.concatenate([piece[:, :shard] for piece in pieces], 1)
            low = jnp.concatenate(
                [piece[:, LANES // 2 : LANES // 2 + shard] for piece in pieces], 1
            )
            raw = jnp.concatenate([top, low], 0)
            natural_ref[block] = raw.T
            x = raw.astype(BF16).astype(F32)
            variance = jnp.sum(x * product(cov, x, EXACT), 0, keepdims=True)
            hat = x * lax.rsqrt(jnp.maximum(variance, 0.0) + 1e-06)
            keys_ref[block] = jnp.concatenate([hat.astype(BF16), filling, constant], 0)

        over(blocks, keys_of)

        def own_of(block):
            for position in range(share):
                own_ref[pl.ds(position * blocks + block, 1), :] = natural_ref[
                    block, pl.ds(position * devices + here, 1), :
                ]

        over(blocks, own_of)
    else:
        lane = iota((devices, LANES), 1) // CH
        held = gathered_ref[...].reshape(devices * blocks, LANES)
        if turned:
            row, column = iota((devices * blocks,) * 2, 0), iota((devices * blocks,) * 2, 1)
            moved = ones_where(column == row % devices * blocks + row // devices)
            held = product(moved, held).astype(BF16)
        natural = held.reshape(blocks, devices, LANES)
        for block in range(blocks):
            keys_ref[block] = jnp.concatenate(
                [
                    jnp.where((lane == position) | (lane == share), natural[block], 0.0).astype(BF16)
                    for position in range(share)
                ],
                0,
            )

    rows = share * blocks
    hat = scaled(own_ref[...], cov).astype(BF16)
    lanes = head_count * SLOTS
    wide = product(hat, ones_where(iota((CH, lanes), 1) % SLOTS == iota((CH, lanes), 0)))
    wide = jnp.where(iota((rows, lanes), 1) % SLOTS == CH, 1.0, wide).astype(BF16)
    row, column = iota((blocks * 8, rows), 0), iota((blocks * 8, rows), 1)
    moved = ones_where((row % 8 == column // blocks) & (row // 8 == column % blocks))
    asked_ref[...] = product(moved, wide)
    asked_mask = iota((head_count * 8, lanes), 0) // 8 == iota((head_count * 8, lanes), 1) // SLOTS
    head_of = iota((8, local_width), 1) // HEAD

    def asked_of(block):
        asked = jnp.concatenate([asked_ref[rows_at(block, 8), :]] * head_count, 0)
        return jnp.where(asked_mask, asked, 0.0).astype(BF16)

    def softmax(scores):
        scores = scores * (1.0 / math.sqrt(HEAD))
        raised = jnp.exp(scores - jnp.max(scores, -1, keepdims=True))
        return (raised / jnp.sum(raised, -1, keepdims=True)).astype(BF16)

    def attend(group):
        members = [group * GROUP + at for at in range(GROUP)]
        queries = [product(asked_of(block), scores_ref[block]).astype(BF16) for block in members]
        meet = product if first else rows_by
        scores = [meet(query, keys_ref[block]) for query, block in zip(queries, members)]
        shares = [softmax(score) for score in scores]
        mix = rows_by if first else product
        mixed = [mix(part, keys_ref[block]).astype(BF16) for part, block in zip(shares, members)]
        mixed = [product(part, values_ref[block]) for part, block in zip(mixed, members)]
        for part, block in zip(mixed, members):
            total = part[0:8]
            for head in range(1, head_count):
                total = jnp.where(head_of == head, part[head * 8 : (head + 1) * 8], total)
            attended_ref[rows_at(block, 8), :] = total

    over(blocks // GROUP, attend)
    row, column = iota((rows, blocks * 8), 0), iota((rows, blocks * 8), 1)
    moved = ones_where((row // blocks == column % 8) & (row % blocks == column // 8))
    attended = product(moved, attended_ref[...].astype(BF16)).astype(BF16)
    term_ref[...] = product(attended, weights_ref[3]).astype(BF16)


def summed(terms):
    total = terms[0][...].astype(F32)
    for term in terms[1:]:
        total = total + term[...].astype(F32)
    return total


def own_half(rows):
    count = rows.shape[0] // 2
    return jnp.where(lax.axis_index("space") == 0, rows[:count], rows[count:])


def attend(half, blocks, query_ref, keys_ref, values_ref, weights_ref):
    rows = query_ref.shape[0]
    local_width = query_ref.shape[1]
    head_count = local_width // HEAD
    kept = slice(0, rows)
    if half is not None:
        rows = rows // 2
        kept = pl.ds(pl.multiple_of(half * rows, rows), rows)
    query = query_ref[kept, :]
    head_of = iota((rows, local_width), 1) // HEAD
    asked = [jnp.where(head_of == head, query, 0.0).astype(BF16) for head in range(head_count)]
    scores = rows_by(jnp.concatenate(asked, 0), keys_ref[kept, :]) * (1.0 / math.sqrt(HEAD))
    row, column = iota(scores.shape, 0) % rows, iota(scores.shape, 1)
    near = (row // blocks == column // blocks) & (jnp.abs(row - column) <= REACH)
    scores = jnp.where(near, scores, -1e30)
    raised = jnp.exp(scores - jnp.max(scores, -1, keepdims=True))
    shares = (raised / jnp.sum(raised, -1, keepdims=True)).astype(BF16)
    mixed = product(shares, values_ref[kept, :])
    total = mixed[0:rows]
    for head in range(1, head_count):
        total = jnp.where(head_of == head, mixed[head * rows : (head + 1) * rows], total)
    return product(total.astype(BF16), weights_ref[3]).astype(BF16)


def temporal_kernel(share, halved, term_count, own_ref, mods_ref, embed_ref, weights_ref, *refs):
    terms, (stream_ref, term_ref, query_ref, keys_ref, values_ref) = (
        refs[:term_count],
        refs[term_count:],
    )
    blocks = mods_ref.shape[0] // PIECES
    stream = product(own_ref[...].astype(BF16), embed_ref[...])
    stream = stream + piece_of(mods_ref, 2, share) * summed(terms)
    stream_ref[...] = own_half(stream) if halved else stream
    normed = layer_norm(stream) * (1.0 + piece_of(mods_ref, 4, share)) + piece_of(mods_ref, 3, share)
    normed = normed.astype(BF16)
    if halved:
        parts = [rows_by(normed, weights_ref[matrix]) for matrix in range(3)]
    else:
        parts = projected(normed, weights_ref)
    for ref, part in zip((query_ref, keys_ref, values_ref), parts):
        ref[...] = part.astype(BF16)
    half = 1 - lax.axis_index("space") if halved else None
    term_ref[...] = attend(half, blocks, query_ref, keys_ref, values_ref, weights_ref)


def kept_kernel(blocks, query_ref, keys_ref, values_ref, weights_ref, term_ref):
    half = lax.axis_index("space")
    term_ref[...] = attend(half, blocks, query_ref, keys_ref, values_ref, weights_ref)


def side_by_side(rows, blocks, share):
    parts = [rows[position * blocks : (position + 1) * blocks] for position in range(share)]
    return jnp.concatenate(parts + [jnp.zeros((blocks, LANES - share * CH), rows.dtype)], 1)


def final_kernel(share, halved, term_count, own_ref, stream_ref, mods_ref, final_ref, sizes_ref, *refs):
    terms, refs = refs[:term_count], refs[term_count:]
    blocks = mods_ref.shape[0] // PIECES
    rows = share * blocks
    own = own_half(own_ref[...]) if halved else own_ref[...]
    stream = stream_ref[...] + piece_of(mods_ref, 5, share) * summed(terms)
    velocity = rows_by(layer_norm(stream).astype(BF16), final_ref[...])
    sizes = jnp.concatenate([sizes_ref[:, :CH]] * share, 0)
    updated = own + sizes * velocity
    moved = jnp.concatenate([updated[1:], updated[:1]], 0)
    return blocks, rows, velocity, moved, refs


def between_kernel(share, term_count, iteration, noise_count, *refs):
    blocks, rows, velocity, moved, refs = final_kernel(share, False, term_count, *refs)
    noises, (cov_ref, velocity_ref, next_ref, sent_ref, noise_ref) = (
        refs[:noise_count],
        refs[noise_count:],
    )
    velocity_ref[...] = velocity
    devices = lax.axis_size("queue")
    here = lax.axis_index("queue")
    if noise_count == 2:
        mine, theirs = noises[0][iteration], noises[1][iteration]
        first = lax.axis_index("space") == 0
        noise = jnp.concatenate(
            [jnp.where(first, mine, theirs), jnp.where(first, theirs, mine)], 1
        )
    else:
        noise = noises[0][iteration]
    noise_ref[...] = noise.T
    next_ref[...] = moved
    for position in range(share):
        next_ref[(position + 1) * blocks - 1 : (position + 1) * blocks, :] = noise_ref[
            pl.ds(position * devices + here, 1), :
        ]
    hat = side_by_side(scaled(next_ref[...], cov_ref[...]), blocks, share)
    hat = jnp.where(iota((blocks, LANES), 1) == share * CH, 1.0, hat)
    sent_ref[...] = jnp.broadcast_to(hat.astype(BF16), sent_ref.shape)


def ending_kernel(share, halved, term_count, *refs):
    blocks, rows, velocity, moved, refs = final_kernel(share, halved, term_count, *refs)
    *earlier, sent_ref = refs
    pick = own_half if halved else lambda rows: rows
    sent_ref[...] = jnp.zeros_like(sent_ref)
    for at, values in enumerate([pick(ref[...]) for ref in earlier] + [velocity, moved]):
        wide = side_by_side(values, blocks, share)
        sent_ref[:, at : at + 1, :] = wide.reshape(blocks, 1, LANES)


def finish_kernel(share, arrived_ref, noise_ref, queue_ref, velocities_ref):
    devices = arrived_ref.shape[0]
    outs = []
    for at in range(STEPS + 1):
        turned = arrived_ref[:, at : at + 1, :].reshape(devices, LANES).T
        parts = [turned[position * CH : (position + 1) * CH] for position in range(share)]
        outs.append(jnp.concatenate(parts, 1))
    for step in range(STEPS):
        velocities_ref[step, 0] = outs[step]
    last = lax.axis_index("queue") == devices - 1
    queue_ref[0] = jnp.where(last, noise_ref[STEPS - 1], outs[STEPS])


def small(limit):
    return pltpu.CompilerParams(vmem_limit_bytes=limit * MIB)


def in_hbm(operands):
    return [pltpu.with_memory_space_constraint(operand, pltpu.HBM) for operand in operands]


def load(weights, first, count):
    shape = (count,) + weights.shape[1:]
    return pl.pallas_call(
        functools.partial(loader_kernel, first),
        out_shape=pltpu.VMEM(shape, weights.dtype),
        in_specs=[pl.BlockSpec(memory_space=pltpu.HBM)],
        out_specs=pl.BlockSpec(memory_space=pltpu.VMEM),
        scratch_shapes=[pltpu.SemaphoreType.DMA((count * BANDS,))],
        compiler_params=small(1),
        cost_estimate=pl.CostEstimate(
            flops=0, bytes_accessed=2 * math.prod(shape), transcendentals=0
        ),
    )(*in_hbm([weights]))


def call(kernel, outs, operands, scratch=(), limit=8, held=True, from_hbm=()):
    specs = [pl.BlockSpec(memory_space=pltpu.VMEM)] * len(operands)
    specs += [pl.BlockSpec(memory_space=pltpu.HBM)] * len(from_hbm)
    if held:
        operands = [pltpu.with_memory_space_constraint(operand, pltpu.VMEM) for operand in operands]
    place = pltpu.VMEM if held else jax.ShapeDtypeStruct
    return pl.pallas_call(
        kernel,
        out_shape=[place(shape, dtype) for shape, dtype in outs],
        in_specs=specs,
        out_specs=[pl.BlockSpec(memory_space=pltpu.VMEM)] * len(outs),
        scratch_shapes=list(scratch),
        compiler_params=small(limit),
    )(*operands, *in_hbm(from_hbm))


def local(
    latents, fresh_noise, levels, modulation_weight, embed_weight, attention_weights, final_weight
):
    devices = lax.axis_size("queue")
    space_count = lax.axis_size("space")
    blocks = devices
    width = embed_weight.shape[1]
    local_width = attention_weights.shape[1]
    head_count = local_width // HEAD
    shard = latents.shape[1]
    tokens = shard * space_count
    share = tokens // devices
    rows = share * blocks
    wide_rows = share * CH + SLOTS
    run = functools.partial(call, limit=12 if rows <= 128 else 40)
    final_rows = final_weight.T
    latents = jnp.swapaxes(latents, 1, 2)
    fresh_noise = jnp.swapaxes(fresh_noise, 1, 2)

    def over_space(x):
        if space_count == 2:
            return [x, lax.ppermute(x, "space", [(0, 1), (1, 0)])]
        gathered = lax.all_gather(x, "space", axis=0, tiled=False)
        return [jnp.sum(gathered.astype(F32), 0)]

    def apart(x, mask):
        count = devices * space_count
        return lax.ppermute(x, ("queue", "space"), [(i, i ^ mask) for i in range(count)])

    def joined(*parts):
        shape = (len(parts) * parts[0].shape[0],) + parts[0].shape[1:]
        return run(join_kernel, [(shape, parts[0].dtype)], list(parts))[0]

    def after(x, *others):
        return lax.optimization_barrier((x, *others))[0]

    def basis(vectors, held):
        return run(
            functools.partial(basis_kernel, len(vectors)),
            [
                ((PIECES * blocks, width), F32),
                ((CH, CH), F32),
                ((3, blocks * CH, local_width), BF16),
                ((3, blocks, local_width), F32),
            ],
            [*vectors, embed_weight, held],
        )

    def forms(seen):
        return run(
            forms_kernel,
            [
                ((blocks, head_count * SLOTS, wide_rows), BF16),
                ((blocks, wide_rows, local_width), BF16),
            ],
            list(seen),
        )

    paired = space_count == 2 and devices == 16
    if paired:
        operands = (levels, modulation_weight, latents, embed_weight)
        vectors, sizes, packed, embed_weight = run(
            opening_kernel,
            [
                ((blocks, modulation_weight.shape[1]), BF16),
                ((blocks, LANES), F32),
                ((1, CH // 2, LANES), F32),
                (embed_weight.shape, BF16),
            ],
            [],
            [
                pltpu.SMEM(levels.shape, levels.dtype),
                pltpu.VMEM(modulation_weight.shape, modulation_weight.dtype),
                pltpu.VMEM(latents.shape, latents.dtype),
                pltpu.SemaphoreType.DMA((len(operands) + BANDS,)),
            ],
            from_hbm=operands,
        )
        vectors = over_space(vectors)
        spatial_weights = load(after(attention_weights, packed), 0, 4)
        gathered = joined(packed, after(apart(packed, 1), spatial_weights))
        arrivals = [apart(gathered, mask) for mask in (2, 4, 6)]
        mods, cov, *seen = basis(vectors, spatial_weights)
        arrivals[-1] = after(arrivals[-1], *seen)
        gathered = joined(gathered, *arrivals)
        arrivals = [apart(gathered, mask) for mask in (8, 16, 24)]
        scores, values = forms(seen)
        arrivals[-1] = after(arrivals[-1], scores)
        gathered = [joined(gathered, *arrivals)]
    else:
        below = jnp.concatenate([jnp.zeros((1,), levels.dtype), levels[:-1]])
        sizes = jnp.broadcast_to(((below - levels).astype(F32) / LEVELS)[:, None], (blocks, LANES))
        part = product(time_features(levels), modulation_weight)
        part = lax.all_gather(part, "space", axis=1, tiled=True).reshape(blocks, PIECES, width)
        vectors = [jnp.swapaxes(part, 0, 1).reshape(PIECES * blocks, width)]
        gap = jnp.zeros((CH // 2, LANES // 2 - shard), F32)
        packed = jnp.concatenate([latents[0, : CH // 2], gap, latents[0, CH // 2 :], gap], 1)
        noises = [lax.all_gather(fresh_noise, "space", axis=2, tiled=True)]
        gathered = lax.all_gather(packed, ("queue", "space"), axis=0, tiled=False)
        gathered = [gathered.reshape(devices * space_count, CH // 2, LANES)]
        spatial_weights = load(attention_weights, 0, 4)
        mods, cov, *seen = basis(vectors, spatial_weights)
        scores, values = forms(seen)
    temporal_weights = None
    own = None
    velocities = []
    for iteration in range(STEPS):
        first = iteration == 0
        outs = [((rows, width), BF16)]
        scratch = [
            pltpu.VMEM((blocks * 8, local_width), F32),
            pltpu.VMEM((blocks * 8, head_count * SLOTS), F32),
            pltpu.VMEM((blocks, wide_rows, tokens) if first else (blocks, tokens, LANES), BF16),
        ]
        if first:
            outs.append(((rows, CH), F32))
            scratch.append(pltpu.VMEM((blocks, tokens, CH), F32))
        spatial_term, *new = run(
            functools.partial(spatial_kernel, first, paired, share),
            outs,
            [*gathered, *([] if first else [own]), cov, scores, values, spatial_weights],
            scratch,
        )
        if first:
            (own,) = new
            held, noise, spatial_term = lax.optimization_barrier(
                (attention_weights, fresh_noise, spatial_term)
            )
            temporal_weights = load(held, 4, 4)
            if paired:
                noises = over_space(noise)
        spatial_terms = over_space(spatial_term)
        if first and paired:
            spatial_terms[-1] = after(spatial_terms[-1], noises[-1])
        last = iteration == STEPS - 1
        halved = last and paired
        held_rows = rows // 2 if halved else rows
        asked = [((rows, local_width), BF16)] * 3
        stream, temporal_term, *asked = run(
            functools.partial(temporal_kernel, share, halved, len(spatial_terms)),
            [((held_rows, width), F32), ((held_rows, width), BF16)] + (asked if halved else []),
            [own, mods, embed_weight, temporal_weights, *spatial_terms],
            [] if halved else [pltpu.VMEM(shape, dtype) for shape, dtype in asked],
        )
        temporal_terms = over_space(temporal_term)
        if halved:
            temporal_terms[:1] = run(
                functools.partial(kept_kernel, blocks),
                [((held_rows, width), BF16)],
                [*asked, temporal_weights],
            )
        operands = [own, stream, mods, final_rows, sizes, *temporal_terms]
        if not last:
            velocity, own, sent = run(
                functools.partial(
                    between_kernel, share, len(temporal_terms), iteration, len(noises)
                ),
                [
                    ((rows, CH), F32),
                    ((rows, CH), F32),
                    ((devices if paired else 1, blocks, LANES), BF16),
                ],
                operands + [*noises, cov],
                [pltpu.VMEM((tokens, CH), F32)],
            )
            velocities.append(velocity)
            if paired:
                gathered = [lax.all_to_all(sent, "queue", 0, 0, tiled=True)]
            else:
                gathered = lax.all_gather(sent[0], "queue", axis=0, tiled=False)
                gathered = [jnp.swapaxes(gathered, 0, 1).reshape(devices * blocks, LANES)]
        else:
            (sent,) = run(
                functools.partial(
                    ending_kernel, share // 2 if halved else share, halved, len(temporal_terms)
                ),
                [((blocks, 8, LANES), F32)],
                operands + velocities,
            )
    arrived = lax.all_to_all(sent, "queue", 0, 0, tiled=True)
    if paired:
        queue_out, velocity_out = run(
            functools.partial(finish_kernel, share // 2),
            [((1, CH, shard), F32), ((STEPS, 1, CH, shard), F32)],
            [arrived, fresh_noise],
            held=False,
        )
    else:
        arrived = arrived[:, : STEPS + 1, : share * CH].reshape(devices, STEPS + 1, share, CH)
        arrived = arrived.transpose(1, 3, 2, 0).reshape(STEPS + 1, CH, tokens)
        arrived = lax.dynamic_slice_in_dim(arrived, lax.axis_index("space") * shard, shard, 2)
        velocity_out = arrived[:STEPS, None]
        last = lax.axis_index("queue") == devices - 1
        queue_out = jnp.where(last, fresh_noise[STEPS - 1], arrived[STEPS])[None]
    return jnp.swapaxes(queue_out, 1, 2), jnp.swapaxes(velocity_out, 2, 3)


def solution(mesh):
    in_specs = (
        P("queue", "space", None),
        P(None, "space", None),
        P(),
        P(None, "space"),
        P(),
        P(None, "space", None),
        P(),
    )
    out_specs = (P("queue", "space", None), P(None, "queue", "space", None))
    return jax.shard_map(local, mesh=mesh, in_specs=in_specs, out_specs=out_specs, check_vma=False)
```

```python
import functools
import math

import jax
import jax.numpy as jnp
from jax import lax
from jax.experimental import pallas as pl
from jax.experimental.pallas import tpu as pltpu
from jax.sharding import PartitionSpec as P

HEAD = 72
FREQ = 256
STEPS = 2
REACH = 4
LEVELS = 1000
CH = 16
PIECES = 6
LANES = 128
SLOTS = 32
GROUP = 16
MIB = 1024 * 1024
F32 = jnp.float32
BF16 = jnp.bfloat16
EXACT = lax.Precision.HIGHEST


def time_features(level_values):
    times = level_values.astype(F32) / LEVELS
    half_size = FREQ // 2
    frequency = jnp.exp(-math.log(10000.0) * jnp.arange(half_size).astype(F32) / half_size)
    angles = (times * 1000.0)[:, None] * frequency[None, :]
    return jnp.concatenate([jnp.cos(angles), jnp.sin(angles)], -1).astype(BF16)


def layer_norm(values):
    average = jnp.mean(values, -1, keepdims=True)
    centred = values - average
    variance = jnp.mean(centred * centred, -1, keepdims=True)
    return centred * lax.rsqrt(variance + 1e-06)


def iota(shape, dimension):
    return lax.broadcasted_iota(jnp.int32, shape, dimension)


def ones_where(condition, dtype=BF16):
    return jnp.where(condition, 1.0, 0.0).astype(dtype)


def rows_by(left, right, precision=None):
    return lax.dot_general(
        left, right, (((1,), (1,)), ((), ())), precision=precision, preferred_element_type=F32
    )


def product(left, right, precision=None):
    return jnp.dot(left, right, precision=precision, preferred_element_type=F32)


def projected(rows, weights_ref):
    local_width, width = weights_ref.shape[1:]
    through = rows_by(rows, weights_ref[0:3].reshape(3 * local_width, width))
    return [through[:, at * local_width : (at + 1) * local_width] for at in range(3)]


def over(count, body):
    if count <= 16:
        for at in range(count):
            body(at)
    else:
        lax.fori_loop(0, count, lambda at, _: body(at), None)


def rows_at(at, size):
    if isinstance(at, int):
        return slice(at * size, (at + 1) * size)
    return pl.ds(pl.multiple_of(at * size, size), size)


def piece_of(mods_ref, piece, share):
    blocks = mods_ref.shape[0] // PIECES
    return jnp.concatenate([mods_ref[piece * blocks : (piece + 1) * blocks, :]] * share, 0)


def scaled(latents, cov):
    x = latents.astype(BF16).astype(F32)
    variance = jnp.sum(x * product(x, cov, EXACT), -1, keepdims=True)
    return x * lax.rsqrt(jnp.maximum(variance, 0.0) + 1e-06)


def loader_kernel(first, weights_ref, held_ref, semaphores):
    copies = [
        pltpu.make_async_copy(weights_ref.at[first + at], held_ref.at[at], semaphores.at[at])
        for at in range(held_ref.shape[0])
    ]
    for copy in copies:
        copy.start()
    for copy in copies:
        copy.wait()


def opening_kernel(
    levels_hbm, weight_hbm, latents_hbm, embed_hbm, vectors_ref, sizes_ref, packed_ref, embed_ref,
    levels_ref, weight_ref, latents_ref, semaphores,
):
    pairs = (
        (levels_hbm, levels_ref),
        (latents_hbm, latents_ref),
        (weight_hbm, weight_ref),
        (embed_hbm, embed_ref),
    )
    copies = [
        pltpu.make_async_copy(source, target, semaphores.at[at])
        for at, (source, target) in enumerate(pairs)
    ]
    for copy in copies:
        copy.start()
    copies[0].wait()
    blocks = vectors_ref.shape[0]
    shape = (blocks, FREQ // 2)
    frequency = jnp.exp(-math.log(10000.0) * iota(shape, 1).astype(F32) / (FREQ // 2))
    row = iota(shape, 0)
    level = jnp.zeros(shape, jnp.int32)
    below = jnp.zeros(shape, jnp.int32)
    for block in range(blocks):
        level = jnp.where(row == block, levels_ref[block], level)
        if block:
            below = jnp.where(row == block, levels_ref[block - 1], below)
    sizes_ref[...] = (below - level).astype(F32) / LEVELS
    angles = (level.astype(F32) / LEVELS * 1000.0) * frequency
    features = jnp.concatenate([jnp.cos(angles), jnp.sin(angles)], -1).astype(BF16)
    copies[1].wait()
    shard = latents_ref.shape[2]
    gap = jnp.zeros((CH // 2, LANES // 2 - shard), F32)
    packed = [latents_ref[0, : CH // 2], gap, latents_ref[0, CH // 2 :], gap]
    packed_ref[0] = jnp.concatenate(packed, 1)
    copies[2].wait()
    vectors_ref[...] = product(features, weight_ref[...]).astype(BF16)
    copies[3].wait()


def join_kernel(*refs):
    *parts, joined_ref = refs
    count = parts[0].shape[0]
    for at, part in enumerate(parts):
        joined_ref[at * count : (at + 1) * count] = part[...]


def basis_kernel(sources, *refs):
    vectors, refs = refs[:sources], refs[sources:]
    embed_ref, weights_ref, mods_ref, cov_ref, rows_ref, last_ref = refs
    blocks = last_ref.shape[1]
    width = weights_ref.shape[2]
    if sources == 2:
        first = lax.axis_index("space") == 0
        mine, theirs = vectors[0][...].astype(F32), vectors[1][...].astype(F32)
        lower = jnp.where(first, mine, theirs)
        upper = jnp.where(first, theirs, mine)
        for piece in range(PIECES):
            part = (lower if piece < 3 else upper)[:, piece % 3 * width : (piece % 3 + 1) * width]
            mods_ref[piece * blocks : (piece + 1) * blocks, :] = part
    else:
        mods_ref[...] = vectors[0][...]
    embed = embed_ref[...].astype(F32)
    centred = embed - jnp.mean(embed, -1, keepdims=True)
    cov_ref[...] = rows_by(centred, centred, EXACT) / width
    scale = 1.0 + mods_ref[blocks : 2 * blocks, :]
    spread = [(centred * scale[block : block + 1, :]).astype(BF16) for block in range(blocks)]
    spread = jnp.concatenate(spread + [mods_ref[0:blocks, :].astype(BF16)], 0)
    for matrix, through in enumerate(projected(spread, weights_ref)):
        rows_ref[matrix] = through[: blocks * CH].astype(BF16)
        last_ref[matrix] = through[blocks * CH :]


def forms_kernel(rows_ref, last_ref, scores_ref, values_ref):
    blocks = scores_ref.shape[0]
    local_width = rows_ref.shape[2]
    share = (LANES - SLOTS) // CH
    head_count = local_width // HEAD
    head_mask = iota((head_count * SLOTS, local_width), 0) // SLOTS == (
        iota((head_count * SLOTS, local_width), 1) // HEAD
    )

    def per_block(block):
        def constant(matrix, size):
            row = last_ref[matrix, pl.ds(block, 1), :]
            return jnp.where(iota((size, local_width), 0) == 0, row, 0.0).astype(BF16)

        def tiled(matrix):
            rows = rows_ref[matrix, rows_at(block, CH), :]
            return jnp.concatenate([rows] * share + [constant(matrix, SLOTS)], 0)

        query = jnp.concatenate([rows_ref[0, rows_at(block, CH), :], constant(0, SLOTS - CH)], 0)
        query = jnp.where(head_mask, jnp.concatenate([query] * head_count, 0), 0.0).astype(BF16)
        scores_ref[block] = rows_by(query, tiled(1)).astype(BF16)
        values_ref[block] = tiled(2)

    over(blocks, per_block)


def spatial_kernel(first, turned, share, *refs):
    if first:
        gathered_ref, cov_ref, scores_ref, values_ref, weights_ref, *refs = refs
    else:
        gathered_ref, own_ref, cov_ref, scores_ref, values_ref, weights_ref, *refs = refs
    if first:
        term_ref, own_ref, attended_ref, asked_ref, keys_ref, natural_ref = refs
    else:
        term_ref, attended_ref, asked_ref, keys_ref = refs
    blocks = scores_ref.shape[0]
    local_width = values_ref.shape[2]
    head_count = local_width // HEAD
    devices = lax.axis_size("queue")
    tokens = share * devices
    here = lax.axis_index("queue")
    cov = cov_ref[...]

    if first:
        parts = gathered_ref.shape[0] // blocks
        shard = tokens // parts
        base = here * parts + lax.axis_index("space") if turned else 0
        filling = jnp.zeros((share * CH - CH, tokens), BF16)
        constant = ones_where(iota((SLOTS, tokens), 0) == 0)

        def keys_of(block):
            pieces = [
                gathered_ref[jnp.bitwise_xor(base, block * parts + part)] for part in range(parts)
            ]
            top = jnp.concatenate([piece[:, :shard] for piece in pieces], 1)
            low = jnp.concatenate(
                [piece[:, LANES // 2 : LANES // 2 + shard] for piece in pieces], 1
            )
            raw = jnp.concatenate([top, low], 0)
            natural_ref[block] = raw.T
            x = raw.astype(BF16).astype(F32)
            variance = jnp.sum(x * product(cov, x, EXACT), 0, keepdims=True)
            hat = x * lax.rsqrt(jnp.maximum(variance, 0.0) + 1e-06)
            keys_ref[block] = jnp.concatenate([hat.astype(BF16), filling, constant], 0)

        over(blocks, keys_of)

        def own_of(block):
            for position in range(share):
                own_ref[pl.ds(position * blocks + block, 1), :] = natural_ref[
                    block, pl.ds(position * devices + here, 1), :
                ]

        over(blocks, own_of)
    else:
        lane = iota((devices, LANES), 1) // CH
        held = gathered_ref[...].reshape(devices * blocks, LANES)
        if turned:
            row, column = iota((devices * blocks,) * 2, 0), iota((devices * blocks,) * 2, 1)
            moved = ones_where(column == row % devices * blocks + row // devices)
            held = product(moved, held).astype(BF16)
        natural = held.reshape(blocks, devices, LANES)
        for block in range(blocks):
            keys_ref[block] = jnp.concatenate(
                [
                    jnp.where((lane == position) | (lane == share), natural[block], 0.0).astype(BF16)
                    for position in range(share)
                ],
                0,
            )

    rows = share * blocks
    hat = (scaled(own_ref[...], cov) if first else own_ref[...]).astype(BF16)
    lanes = head_count * SLOTS
    wide = product(hat, ones_where(iota((CH, lanes), 1) % SLOTS == iota((CH, lanes), 0)))
    wide = jnp.where(iota((rows, lanes), 1) % SLOTS == CH, 1.0, wide).astype(BF16)
    row, column = iota((blocks * 8, rows), 0), iota((blocks * 8, rows), 1)
    moved = ones_where((row % 8 == column // blocks) & (row // 8 == column % blocks))
    asked_ref[...] = product(moved, wide)
    asked_mask = iota((head_count * 8, lanes), 0) // 8 == iota((head_count * 8, lanes), 1) // SLOTS
    head_of = iota((8, local_width), 1) // HEAD

    def asked_of(block):
        asked = jnp.concatenate([asked_ref[rows_at(block, 8), :]] * head_count, 0)
        return jnp.where(asked_mask, asked, 0.0).astype(BF16)

    def softmax(scores):
        scores = scores * (1.0 / math.sqrt(HEAD))
        raised = jnp.exp(scores - jnp.max(scores, -1, keepdims=True))
        return (raised / jnp.sum(raised, -1, keepdims=True)).astype(BF16)

    def attend(group):
        members = [group * GROUP + at for at in range(GROUP)]
        queries = [product(asked_of(block), scores_ref[block]).astype(BF16) for block in members]
        meet = product if first else rows_by
        scores = [meet(query, keys_ref[block]) for query, block in zip(queries, members)]
        shares = [softmax(score) for score in scores]
        mix = rows_by if first else product
        mixed = [mix(part, keys_ref[block]).astype(BF16) for part, block in zip(shares, members)]
        mixed = [product(part, values_ref[block]) for part, block in zip(mixed, members)]
        for part, block in zip(mixed, members):
            total = part[0:8]
            for head in range(1, head_count):
                total = jnp.where(head_of == head, part[head * 8 : (head + 1) * 8], total)
            attended_ref[rows_at(block, 8), :] = total

    over(blocks // GROUP, attend)
    row, column = iota((rows, blocks * 8), 0), iota((rows, blocks * 8), 1)
    moved = ones_where((row // blocks == column % 8) & (row % blocks == column // 8))
    attended = product(moved, attended_ref[...].astype(BF16)).astype(BF16)
    term_ref[...] = product(attended, weights_ref[3]).astype(BF16)


def summed(terms):
    total = terms[0][...].astype(F32)
    for term in terms[1:]:
        total = total + term[...].astype(F32)
    return total


def own_half(rows):
    count = rows.shape[0] // 2
    return jnp.where(lax.axis_index("space") == 0, rows[:count], rows[count:])


def attend(half, blocks, query_ref, keys_ref, values_ref, weights_ref):
    rows = query_ref.shape[0]
    local_width = query_ref.shape[1]
    head_count = local_width // HEAD
    kept = slice(0, rows)
    if half is not None:
        rows = rows // 2
        kept = pl.ds(pl.multiple_of(half * rows, rows), rows)
    query = query_ref[kept, :]
    head_of = iota((rows, local_width), 1) // HEAD
    asked = [jnp.where(head_of == head, query, 0.0).astype(BF16) for head in range(head_count)]
    scores = rows_by(jnp.concatenate(asked, 0), keys_ref[kept, :]) * (1.0 / math.sqrt(HEAD))
    row, column = iota(scores.shape, 0) % rows, iota(scores.shape, 1)
    near = (row // blocks == column // blocks) & (jnp.abs(row - column) <= REACH)
    scores = jnp.where(near, scores, -1e30)
    raised = jnp.exp(scores - jnp.max(scores, -1, keepdims=True))
    shares = (raised / jnp.sum(raised, -1, keepdims=True)).astype(BF16)
    mixed = product(shares, values_ref[kept, :])
    total = mixed[0:rows]
    for head in range(1, head_count):
        total = jnp.where(head_of == head, mixed[head * rows : (head + 1) * rows], total)
    return product(total.astype(BF16), weights_ref[3]).astype(BF16)


def temporal_kernel(share, halved, term_count, own_ref, mods_ref, embed_ref, weights_ref, *refs):
    terms, (stream_ref, term_ref, query_ref, keys_ref, values_ref) = (
        refs[:term_count],
        refs[term_count:],
    )
    blocks = mods_ref.shape[0] // PIECES
    stream = product(own_ref[...].astype(BF16), embed_ref[...])
    stream = stream + piece_of(mods_ref, 2, share) * summed(terms)
    stream_ref[...] = own_half(stream) if halved else stream
    normed = layer_norm(stream) * (1.0 + piece_of(mods_ref, 4, share)) + piece_of(mods_ref, 3, share)
    normed = normed.astype(BF16)
    if halved:
        parts = [rows_by(normed, weights_ref[matrix]) for matrix in range(3)]
    else:
        parts = projected(normed, weights_ref)
    for ref, part in zip((query_ref, keys_ref, values_ref), parts):
        ref[...] = part.astype(BF16)
    half = 1 - lax.axis_index("space") if halved else None
    term_ref[...] = attend(half, blocks, query_ref, keys_ref, values_ref, weights_ref)


def kept_kernel(blocks, query_ref, keys_ref, values_ref, weights_ref, term_ref):
    half = lax.axis_index("space")
    term_ref[...] = attend(half, blocks, query_ref, keys_ref, values_ref, weights_ref)


def side_by_side(rows, blocks, share):
    parts = [rows[position * blocks : (position + 1) * blocks] for position in range(share)]
    return jnp.concatenate(parts + [jnp.zeros((blocks, LANES - share * CH), rows.dtype)], 1)


def final_kernel(share, halved, term_count, own_ref, stream_ref, mods_ref, final_ref, sizes_ref, *refs):
    terms, refs = refs[:term_count], refs[term_count:]
    blocks = mods_ref.shape[0] // PIECES
    rows = share * blocks
    own = own_half(own_ref[...]) if halved else own_ref[...]
    stream = stream_ref[...] + piece_of(mods_ref, 5, share) * summed(terms)
    velocity = rows_by(layer_norm(stream).astype(BF16), final_ref[...])
    sizes = jnp.concatenate([sizes_ref[:, :CH]] * share, 0)
    updated = own + sizes * velocity
    moved = jnp.concatenate([updated[1:], updated[:1]], 0)
    return blocks, rows, velocity, moved, refs


def between_kernel(share, term_count, iteration, noise_count, *refs):
    blocks, rows, velocity, moved, refs = final_kernel(share, False, term_count, *refs)
    noises, (cov_ref, velocity_ref, next_ref, hat_ref, sent_ref, noise_ref) = (
        refs[:noise_count],
        refs[noise_count:],
    )
    velocity_ref[...] = velocity
    devices = lax.axis_size("queue")
    here = lax.axis_index("queue")
    if noise_count == 2:
        mine, theirs = noises[0][iteration], noises[1][iteration]
        first = lax.axis_index("space") == 0
        noise = jnp.concatenate(
            [jnp.where(first, mine, theirs), jnp.where(first, theirs, mine)], 1
        )
    else:
        noise = noises[0][iteration]
    noise_ref[...] = noise.T
    next_ref[...] = moved
    for position in range(share):
        next_ref[(position + 1) * blocks - 1 : (position + 1) * blocks, :] = noise_ref[
            pl.ds(position * devices + here, 1), :
        ]
    hat = scaled(next_ref[...], cov_ref[...])
    hat_ref[...] = hat
    hat = side_by_side(hat, blocks, share)
    hat = jnp.where(iota((blocks, LANES), 1) == share * CH, 1.0, hat)
    sent_ref[...] = jnp.broadcast_to(hat.astype(BF16), sent_ref.shape)


def ending_kernel(share, halved, term_count, *refs):
    blocks, rows, velocity, moved, refs = final_kernel(share, halved, term_count, *refs)
    *earlier, sent_ref = refs
    pick = own_half if halved else lambda rows: rows
    sent_ref[...] = jnp.zeros_like(sent_ref)
    for at, values in enumerate([pick(ref[...]) for ref in earlier] + [velocity, moved]):
        wide = side_by_side(values, blocks, share)
        sent_ref[:, at : at + 1, :] = wide.reshape(blocks, 1, LANES)


def finish_kernel(share, arrived_ref, noise_ref, queue_ref, velocities_ref):
    devices = arrived_ref.shape[0]
    outs = []
    for at in range(STEPS + 1):
        turned = arrived_ref[:, at : at + 1, :].reshape(devices, LANES).T
        parts = [turned[position * CH : (position + 1) * CH] for position in range(share)]
        outs.append(jnp.concatenate(parts, 1))
    for step in range(STEPS):
        velocities_ref[step, 0] = outs[step]
    last = lax.axis_index("queue") == devices - 1
    queue_ref[0] = jnp.where(last, noise_ref[STEPS - 1], outs[STEPS])


def small(limit):
    return pltpu.CompilerParams(vmem_limit_bytes=limit * MIB)


def in_hbm(operands):
    return [pltpu.with_memory_space_constraint(operand, pltpu.HBM) for operand in operands]


def load(weights, first, count):
    shape = (count,) + weights.shape[1:]
    return pl.pallas_call(
        functools.partial(loader_kernel, first),
        out_shape=pltpu.VMEM(shape, weights.dtype),
        in_specs=[pl.BlockSpec(memory_space=pltpu.HBM)],
        out_specs=pl.BlockSpec(memory_space=pltpu.VMEM),
        scratch_shapes=[pltpu.SemaphoreType.DMA((count,))],
        compiler_params=small(1),
        cost_estimate=pl.CostEstimate(
            flops=0, bytes_accessed=2 * math.prod(shape), transcendentals=0
        ),
    )(*in_hbm([weights]))


def call(kernel, outs, operands, scratch=(), limit=8, held=True, from_hbm=()):
    specs = [pl.BlockSpec(memory_space=pltpu.VMEM)] * len(operands)
    specs += [pl.BlockSpec(memory_space=pltpu.HBM)] * len(from_hbm)
    if held:
        operands = [pltpu.with_memory_space_constraint(operand, pltpu.VMEM) for operand in operands]
    place = pltpu.VMEM if held else jax.ShapeDtypeStruct
    return pl.pallas_call(
        kernel,
        out_shape=[place(shape, dtype) for shape, dtype in outs],
        in_specs=specs,
        out_specs=[pl.BlockSpec(memory_space=pltpu.VMEM)] * len(outs),
        scratch_shapes=list(scratch),
        compiler_params=small(limit),
    )(*operands, *in_hbm(from_hbm))


def local(
    latents, fresh_noise, levels, modulation_weight, embed_weight, attention_weights, final_weight
):
    devices = lax.axis_size("queue")
    space_count = lax.axis_size("space")
    blocks = devices
    width = embed_weight.shape[1]
    local_width = attention_weights.shape[1]
    head_count = local_width // HEAD
    shard = latents.shape[1]
    tokens = shard * space_count
    share = tokens // devices
    rows = share * blocks
    wide_rows = share * CH + SLOTS
    run = functools.partial(call, limit=12 if rows <= 128 else 40)
    final_rows = final_weight.T
    latents = jnp.swapaxes(latents, 1, 2)
    fresh_noise = jnp.swapaxes(fresh_noise, 1, 2)

    def over_space(x):
        if space_count == 2:
            return [x, lax.ppermute(x, "space", [(0, 1), (1, 0)])]
        gathered = lax.all_gather(x, "space", axis=0, tiled=False)
        return [jnp.sum(gathered.astype(F32), 0)]

    def apart(x, mask):
        count = devices * space_count
        return lax.ppermute(x, ("queue", "space"), [(i, i ^ mask) for i in range(count)])

    def joined(*parts):
        shape = (len(parts) * parts[0].shape[0],) + parts[0].shape[1:]
        return run(join_kernel, [(shape, parts[0].dtype)], list(parts))[0]

    def after(x, *others):
        return lax.optimization_barrier((x, *others))[0]

    def basis(vectors, held):
        return run(
            functools.partial(basis_kernel, len(vectors)),
            [
                ((PIECES * blocks, width), F32),
                ((CH, CH), F32),
                ((3, blocks * CH, local_width), BF16),
                ((3, blocks, local_width), F32),
            ],
            [*vectors, embed_weight, held],
        )

    def forms(seen):
        return run(
            forms_kernel,
            [
                ((blocks, head_count * SLOTS, wide_rows), BF16),
                ((blocks, wide_rows, local_width), BF16),
            ],
            list(seen),
        )

    paired = space_count == 2 and devices == 16
    if paired:
        operands = (levels, modulation_weight, latents, embed_weight)
        vectors, sizes, packed, embed_weight = run(
            opening_kernel,
            [
                ((blocks, modulation_weight.shape[1]), BF16),
                ((blocks, LANES), F32),
                ((1, CH // 2, LANES), F32),
                (embed_weight.shape, BF16),
            ],
            [],
            [
                pltpu.SMEM(levels.shape, levels.dtype),
                pltpu.VMEM(modulation_weight.shape, modulation_weight.dtype),
                pltpu.VMEM(latents.shape, latents.dtype),
                pltpu.SemaphoreType.DMA((len(operands),)),
            ],
            from_hbm=operands,
        )
        vectors = over_space(vectors)
        spatial_weights = load(after(attention_weights, packed), 0, 4)
        gathered = joined(packed, after(apart(packed, 1), spatial_weights))
        arrivals = [apart(gathered, mask) for mask in (2, 4, 6)]
        mods, cov, *seen = basis(vectors, spatial_weights)
        arrivals[-1] = after(arrivals[-1], *seen)
        gathered = joined(gathered, *arrivals)
        arrivals = [apart(gathered, mask) for mask in (8, 16, 24)]
        scores, values = forms(seen)
        arrivals[-1] = after(arrivals[-1], scores)
        gathered = [joined(gathered, *arrivals)]
    else:
        below = jnp.concatenate([jnp.zeros((1,), levels.dtype), levels[:-1]])
        sizes = jnp.broadcast_to(((below - levels).astype(F32) / LEVELS)[:, None], (blocks, LANES))
        part = product(time_features(levels), modulation_weight)
        part = lax.all_gather(part, "space", axis=1, tiled=True).reshape(blocks, PIECES, width)
        vectors = [jnp.swapaxes(part, 0, 1).reshape(PIECES * blocks, width)]
        gap = jnp.zeros((CH // 2, LANES // 2 - shard), F32)
        packed = jnp.concatenate([latents[0, : CH // 2], gap, latents[0, CH // 2 :], gap], 1)
        noises = [lax.all_gather(fresh_noise, "space", axis=2, tiled=True)]
        gathered = lax.all_gather(packed, ("queue", "space"), axis=0, tiled=False)
        gathered = [gathered.reshape(devices * space_count, CH // 2, LANES)]
        spatial_weights = load(attention_weights, 0, 4)
        mods, cov, *seen = basis(vectors, spatial_weights)
        scores, values = forms(seen)
    temporal_weights = None
    own = None
    velocities = []
    for iteration in range(STEPS):
        first = iteration == 0
        outs = [((rows, width), BF16)]
        scratch = [
            pltpu.VMEM((blocks * 8, local_width), F32),
            pltpu.VMEM((blocks * 8, head_count * SLOTS), F32),
            pltpu.VMEM((blocks, wide_rows, tokens) if first else (blocks, tokens, LANES), BF16),
        ]
        if first:
            outs.append(((rows, CH), F32))
            scratch.append(pltpu.VMEM((blocks, tokens, CH), F32))
        spatial_term, *new = run(
            functools.partial(spatial_kernel, first, paired, share),
            outs,
            [*gathered, *([] if first else [hat]), cov, scores, values, spatial_weights],
            scratch,
        )
        if first:
            (own,) = new
            held, noise, spatial_term = lax.optimization_barrier(
                (attention_weights, fresh_noise, spatial_term)
            )
            temporal_weights = load(held, 4, 4)
            if paired:
                noises = over_space(noise)
        spatial_terms = over_space(spatial_term)
        if first and paired:
            spatial_terms[-1] = after(spatial_terms[-1], noises[-1])
        last = iteration == STEPS - 1
        halved = last and paired
        held_rows = rows // 2 if halved else rows
        asked = [((rows, local_width), BF16)] * 3
        stream, temporal_term, *asked = run(
            functools.partial(temporal_kernel, share, halved, len(spatial_terms)),
            [((held_rows, width), F32), ((held_rows, width), BF16)] + (asked if halved else []),
            [own, mods, embed_weight, temporal_weights, *spatial_terms],
            [] if halved else [pltpu.VMEM(shape, dtype) for shape, dtype in asked],
        )
        temporal_terms = over_space(temporal_term)
        if halved:
            temporal_terms[:1] = run(
                functools.partial(kept_kernel, blocks),
                [((held_rows, width), BF16)],
                [*asked, temporal_weights],
            )
        operands = [own, stream, mods, final_rows, sizes, *temporal_terms]
        if not last:
            velocity, own, hat, sent = run(
                functools.partial(
                    between_kernel, share, len(temporal_terms), iteration, len(noises)
                ),
                [((rows, CH), F32)] * 3
                + [
                    ((devices if paired else 1, blocks, LANES), BF16),
                ],
                operands + [*noises, cov],
                [pltpu.VMEM((tokens, CH), F32)],
            )
            velocities.append(velocity)
            if paired:
                gathered = [lax.all_to_all(sent, "queue", 0, 0, tiled=True)]
            else:
                gathered = lax.all_gather(sent[0], "queue", axis=0, tiled=False)
                gathered = [jnp.swapaxes(gathered, 0, 1).reshape(devices * blocks, LANES)]
        else:
            (sent,) = run(
                functools.partial(
                    ending_kernel, share // 2 if halved else share, halved, len(temporal_terms)
                ),
                [((blocks, 8, LANES), F32)],
                operands + velocities,
            )
    arrived = lax.all_to_all(sent, "queue", 0, 0, tiled=True)
    if paired:
        queue_out, velocity_out = run(
            functools.partial(finish_kernel, share // 2),
            [((1, CH, shard), F32), ((STEPS, 1, CH, shard), F32)],
            [arrived, fresh_noise],
            held=False,
        )
    else:
        arrived = arrived[:, : STEPS + 1, : share * CH].reshape(devices, STEPS + 1, share, CH)
        arrived = arrived.transpose(1, 3, 2, 0).reshape(STEPS + 1, CH, tokens)
        arrived = lax.dynamic_slice_in_dim(arrived, lax.axis_index("space") * shard, shard, 2)
        velocity_out = arrived[:STEPS, None]
        last = lax.axis_index("queue") == devices - 1
        queue_out = jnp.where(last, fresh_noise[STEPS - 1], arrived[STEPS])[None]
    return jnp.swapaxes(queue_out, 1, 2), jnp.swapaxes(velocity_out, 2, 3)


def solution(mesh):
    in_specs = (
        P("queue", "space", None),
        P(None, "space", None),
        P(),
        P(None, "space"),
        P(),
        P(None, "space", None),
        P(),
    )
    out_specs = (P("queue", "space", None), P(None, "queue", "space", None))
    return jax.shard_map(local, mesh=mesh, in_specs=in_specs, out_specs=out_specs, check_vma=False)
```
